256 devices in a mesh: wide: 64 (over z_lo, y, x, core), narrow: 4 (over z_hi).
Axes of the slice: x: 4, y: 4, z: 8 (z_hi: 4, z_lo: 2; z = z_hi * 2 + z_lo), core: 2. Of those that a mesh axis runs over, the one named last changes fastest.
Arguments:
- divergence: float32 [512, 32, 512], P('wide', None, 'narrow'), may hold values from -6 to 6
- pressure_start: float32 [512, 32, 512], P('wide', None, 'narrow'), may hold values from -3 to 3
- phase: int32 [512, 32, 512], P('wide', None, 'narrow'), may hold values 0 or 1
- velocity_cot: float32 [3, 512, 32, 512], P(None, 'wide', None, 'narrow'), may hold values from -6 to 6
Outputs:
- grad_divergence: float32 [512, 32, 512], P('wide', None, 'narrow')
- grad_pressure: float32 [512, 32, 512], P('wide', None, 'narrow')
- grad_faces: float32 [3, 512, 32, 512], P(None, 'wide', None, 'narrow')
The draws below stay inside these ranges and needn't reach their ends.
Inputs may be any that keep to these rules, and one draw needn't show every extreme that they name: `phase`: 0 marks a liquid cell, 1 a gas cell.
All inputs are finite; a program needn't handle non-finite values. No bound on the sum of `phase` on one device may be relied on, other than what follows from the above.
Results may differ from the reference program's by a relative error of at most 0.0003.
Values sent between devices are 32-bit elements; how exact they have to be, the bound alone decides.
A program may use at most 64 MiB of HBM per device.

```python
import math
import jax
import jax.numpy as jnp
from jax import lax

NY = 32
SWEEPS = 6
NX = 512
NZ = 512


def touch_ends(values, key, low, high):
    longest = values.shape.index(max(values.shape))
    spots = []
    for shift in (0, 1):
        where = [jax.random.randint(jax.random.fold_in(key, axis), (), 0, length) for axis, length in enumerate(values.shape)]
        where[longest] = (where[longest] + shift) % values.shape[longest]
        spots.append(tuple(where))
    return values.at[spots[0]].set(low).at[spots[1]].set(high)


def levels(key, extent, shards, low, high):
    level, own = 1.0, jax.random.fold_in(key, 6)
    for axis_at, shards_of in shards:
        draws = jnp.exp(jax.random.uniform(jax.random.fold_in(own, axis_at), (shards_of,), jnp.float32, low / len(shards), high / len(shards)))
        level = level * jnp.repeat(draws, extent[axis_at] // shards_of).reshape([-1 if axis == axis_at else 1 for axis in range(len(extent))])
    return level


def gaussian(rng, shape, width, most, split=(), held_as=jnp.bfloat16):
    level = levels(rng, shape, split, -0.22, 0.18) if split else 1.0
    drawn = jax.random.normal(rng, shape, jnp.float32) * width * level
    return jnp.minimum(jnp.maximum(drawn, -most), most).astype(held_as)


def setup_inputs(seed: int = 0) -> dict:
    key_of = jax.random.split(jax.random.key(seed), 5)
    divergence = gaussian(key_of[0], (NX, NY, NZ), 1.0, 6.0, ((0, 64), (2, 4)), jnp.float32)
    pressure_start = gaussian(key_of[1], (NX, NY, NZ), 0.5, 3.0, ((0, 64), (2, 4)), jnp.float32)
    phase = touch_ends((jax.random.randint(key_of[2], (NX, NY, NZ), 0, 3) < 1).astype(jnp.int32), jax.random.fold_in(key_of[2], 1), 0, 1)
    velocity_cot = gaussian(key_of[3], (3, NX, NY, NZ), 1.0, 6.0, ((1, 64), (3, 4)), jnp.float32)
    return {"divergence": divergence, "pressure_start": pressure_start, "phase": phase, "velocity_cot": velocity_cot}


gas_density = 0.25
lower_bound = 0.25
upper_bound = 2.0

def chebyshev_weights(count):
    center = 0.5 * (upper_bound + lower_bound)
    radius = 0.5 * (upper_bound - lower_bound)
    roots = [center + radius * math.cos(math.pi * (2 * number + 1) / (2 * count)) for number in range(count)]
    order = []
    for number in range(count // 2):
        order.append(number)
        order.append(count - 1 - number)
    if count % 2 == 1:
        order.append(count // 2)
    return [1.0 / roots[position] for position in order]

def shift_up(array, axis_dim):
    length = array.shape[axis_dim]
    zeros = jnp.zeros_like(lax.slice_in_dim(array, 0, 1, axis=axis_dim))
    return jnp.concatenate([lax.slice_in_dim(array, 1, length, axis=axis_dim), zeros], axis=axis_dim)

def shift_down(array, axis_dim):
    length = array.shape[axis_dim]
    zeros = jnp.zeros_like(lax.slice_in_dim(array, 0, 1, axis=axis_dim))
    return jnp.concatenate([zeros, lax.slice_in_dim(array, 0, length - 1, axis=axis_dim)], axis=axis_dim)

def reference(divergence, pressure_start, phase, velocity_cot):
    density = jnp.where(phase == 1, gas_density, 1.0).astype(jnp.float32)
    upper = []
    edges = []
    for axis_dim in range(3):
        above = shift_up(density, axis_dim)
        upper.append(2.0 / (density + jnp.where(above > 0.0, above, density)))
        below = shift_down(density, axis_dim)
        edges.append(jnp.where(below > 0.0, 0.0, 1.0 / density).astype(jnp.float32))
    weights = chebyshev_weights(SWEEPS)

    def make_sweep(weight):

        def sweep(pressure, source, faces):
            lower = [shift_down(faces[axis_dim], axis_dim) + edges[axis_dim] for axis_dim in range(3)]
            diag = faces[0] + lower[0] + faces[1] + lower[1] + faces[2] + lower[2]
            applied = jnp.zeros_like(pressure)
            for axis_dim in range(3):
                applied = applied + faces[axis_dim] * (pressure - shift_up(pressure, axis_dim))
                applied = applied + lower[axis_dim] * (pressure - shift_down(pressure, axis_dim))
            return pressure + weight * (source - applied) / diag
        return jax.checkpoint(sweep)

    def forward(source, start, faces):
        pressure = start
        for weight in weights:
            pressure = make_sweep(weight)(pressure, source, faces)
        return jnp.stack([-faces[axis_dim] * (shift_up(pressure, axis_dim) - pressure) for axis_dim in range(3)])
    result, pullback = jax.vjp(forward, divergence, pressure_start, tuple(upper))
    grad_source, grad_start, grad_upper = pullback(velocity_cot)
    return (grad_source, grad_start, jnp.stack(list(grad_upper)))
```

```python
import math

import jax
import jax.numpy as jnp
from jax import lax
from jax.experimental import pallas as pl
from jax.experimental.pallas import tpu as pltpu
from jax.sharding import PartitionSpec as P

SWEEPS = 6
CENTER, RADIUS = 1.125, 0.875
PAD = 16
ROWS = 160
NZ = 128
NY = 32
F32 = jnp.float32
MESH = pl.DeviceIdType.MESH
XU, XD, YU, YD, ZU, ZD = range(6)


def chebyshev_weights():
    roots = [CENTER + RADIUS * math.cos(math.pi * (2 * m + 1) / (2 * SWEEPS)) for m in range(SWEEPS)]
    order = []
    for m in range(SWEEPS // 2):
        order += [m, SWEEPS - 1 - m]
    return [1.0 / roots[m] for m in order]


W = chebyshev_weights()


def lanes(rows):
    return lax.broadcasted_iota(jnp.int32, (rows, 128), 1)


def x_up(tile, after, lane):
    return pltpu.roll(tile if after is None else jnp.where(lane < 32, after, tile), 96, 1)


def x_down(tile, before, lane):
    return pltpu.roll(tile if before is None else jnp.where(lane >= 96, before, tile), 32, 1)


def y_up(tile):
    return pltpu.roll(tile, 127, 1)


def y_down(tile):
    return pltpu.roll(tile, 1, 1)


def turned(block):
    return jnp.transpose(block.reshape(128, 128))


def local_sums(ph, ps, dv, vc, lam, res):
    row = lax.broadcasted_iota(jnp.int32, (NY, NZ), 0)
    lane = lax.broadcasted_iota(jnp.int32, (NY, NZ), 1)
    top, bottom, inner = row == NY - 1, row == 0, lane < NZ - 1
    before_lam = before_res = None
    here = ph[0].astype(F32)
    for x in range(8):
        a = here
        base, slope = 1.0 + 0.6 * a, 0.6 + 1.8 * a
        p = ps[x]
        face_y = base + slope * jnp.where(top, a, pltpu.roll(a, NY - 1, 0))
        face_z = jnp.where(inner, base + slope * pltpu.roll(a, NZ - 1, 1), 0.0)
        flux_y = face_y * vc[1, x]
        flux_z = face_z * vc[2, x]
        flow_y = face_y * (p - jnp.where(top, 0.0, pltpu.roll(p, NY - 1, 0)))
        flow_z = face_z * (p - pltpu.roll(p, NZ - 1, 1))
        total = flux_y - jnp.where(bottom, 0.0, pltpu.roll(flux_y, 1, 0)) + flux_z - pltpu.roll(flux_z, 1, 1)
        lower = jnp.where(bottom, -(1.0 + 3.0 * a) * p, pltpu.roll(flow_y, 1, 0))
        rest = dv[x] - (flow_y - lower) - (flow_z - pltpu.roll(flow_z, 1, 1))
        if x > 0:
            total = total - before_lam
            rest = rest + before_res
        if x < 7:
            here = ph[x + 1].astype(F32)
            face_x = base + slope * here
            before_lam = face_x * vc[0, x]
            before_res = face_x * (p - ps[x + 1])
            total = total + before_lam
            rest = rest - before_res
        lam[x] = total
        res[x] = rest


def coefficients(phe, coef, inv, diag, row, rows):
    lane = lanes(rows)
    last, first = (lane & 31) == 31, (lane & 31) == 0
    cur = [phe[c, pl.ds(row, rows), :] for c in range(6)]
    for c in range(6):
        a = cur[c]
        near = [
            x_up(a, cur[c + 1] if c < 5 else None, lane),
            x_down(a, cur[c - 1] if c > 0 else None, lane),
            jnp.where(last, a, y_up(a)),
            jnp.where(first, a, y_down(a)),
            phe[c, pl.ds(row + 1, rows), :],
            phe[c, pl.ds(row - 1, rows), :],
        ]
        near = [b if k in (YU, YD) else jnp.where(b > 1.5, a, b) for k, b in enumerate(near)]
        base, slope = 1.0 + 0.6 * a, 0.6 + 1.8 * a
        total = 6.0 * base + slope * ((near[0] + near[1]) + (near[2] + near[3]) + (near[4] + near[5]))
        inverse = jnp.where(a > 1.5, 0.0, 1.0 / total)
        inv[c, pl.ds(row, rows), :] = inverse
        base, slope = base * inverse, slope * inverse
        for k in range(6):
            value = base + slope * near[k]
            if k == YU:
                value = jnp.where(last, 0.0, value)
            if k == YD:
                value = jnp.where(first, 0.0, value)
            coef[k, c, pl.ds(row, rows), :] = value
        if c in (2, 3):
            diag[c - 2, pl.ds(row, rows), :] = total


def starts(lame, rese, inv, coef, near_edge, own_edge, s5, e0, row, rows):
    lane = lanes(rows)
    low, high = lane < 32, lane >= 96
    ne = near_edge[pl.ds(row, rows), :]
    step = ne - own_edge[pl.ds(row, rows), :]
    for c in range(6):
        i = inv[c, pl.ds(row, rows), :]
        lam = i * lame[c, pl.ds(row, rows), :]
        res = i * rese[c, pl.ds(row, rows), :]
        if c == 1:
            cf = coef[XU, c, pl.ds(row, rows), :]
            lam = lam + jnp.where(high, cf * pltpu.roll(ne, 64, 1), 0.0)
            res = res - jnp.where(high, cf * pltpu.roll(step, 96, 1), 0.0)
        elif c == 2:
            cf = coef[XD, c, pl.ds(row, rows), :]
            lam = lam - jnp.where(low, cf * pltpu.roll(ne, 96, 1), 0.0)
            res = res + jnp.where(low, cf * step, 0.0)
        elif c == 3:
            cf = coef[XU, c, pl.ds(row, rows), :]
            lam = lam + jnp.where(high, cf * ne, 0.0)
            res = res + jnp.where(high, cf * pltpu.roll(step, 32, 1), 0.0)
        elif c == 4:
            cf = coef[XD, c, pl.ds(row, rows), :]
            lam = lam - jnp.where(low, cf * pltpu.roll(ne, 32, 1), 0.0)
            res = res - jnp.where(low, cf * pltpu.roll(step, 64, 1), 0.0)
        s5[c, pl.ds(row, rows), :] = W[5] * lam
        e0[c, pl.ds(row, rows), :] = W[0] * res


def exchange(
    dv_hbm, ps_hbm, ph_hbm, vc_hbm,
    coef, s5, e0, pe, diag, vt,
    ph, ps, dv, vc, lam, res, rx_ph, rx_lam, rx_res, ne, edge_out, zs, rz, rd,
    phe, lame, rese, inv, near_edge, own_edge,
    in_sem, send_x, recv_x, send_z, recv_z, send_d, recv_d,
):
    w, n = lax.axis_index("wide"), lax.axis_index("narrow")
    nw, nn = lax.axis_size("wide"), lax.axis_size("narrow")
    x_after, x_before = (lax.rem(w + 1, nw), n), (lax.rem(w + nw - 1, nw), n)
    z_after, z_before = (w, lax.rem(n + 1, nn)), (w, lax.rem(n + nn - 1, nn))
    barrier = pltpu.get_barrier_semaphore()
    for device in (x_after, x_before, z_after, z_before):
        pl.semaphore_signal(barrier, inc=1, device_id=device, device_id_type=MESH)
    loads = [
        pltpu.make_async_copy(src, dst, in_sem.at[k])
        for k, (src, dst) in enumerate(((ph_hbm, ph), (ps_hbm, ps), (dv_hbm, dv), (vc_hbm, vc)))
    ]
    for load in loads:
        load.start()
    zero = jnp.zeros((NY, NZ), F32)
    rx_ph[0, 0] = jnp.zeros((NY, NZ), jnp.int32)
    rx_ph[1, 7] = jnp.zeros((NY, NZ), jnp.int32)
    for k in (0, 1):
        rx_lam[0, k] = zero
        rx_res[0, k] = zero
        rx_lam[1, 6 + k] = zero
        rx_res[1, 6 + k] = zero
    rx_res[0, 2] = zero
    for c in range(6):
        for r in (0, 152):
            phe[c, r : r + 8, :] = jnp.zeros((8, 128), F32)
            s5[c, r : r + 8, :] = jnp.zeros((8, 128), F32)
            e0[c, r : r + 8, :] = jnp.zeros((8, 128), F32)
    for load in loads:
        load.wait()

    local_sums(ph, ps, dv, vc, lam, res)
    main = slice(PAD, PAD + NZ)
    for j in range(2):
        part = slice(4 * j, 4 * j + 4)
        phe[2 + j, main, :] = turned(ph[part].astype(F32))
        lame[2 + j, main, :] = turned(lam[part])
        rese[2 + j, main, :] = turned(res[part])
        pe[j, main, :] = turned(ps[part])
        for a in range(3):
            vt[a, j] = turned(vc[a, part])
    own_edge[main, :] = turned(jnp.stack([ps[0], vc[0, 7], ps[7], vc[0, 7]]))
    edge_out[0] = ps[7]
    edge_out[1] = vc[0, 7]
    ne[3] = vc[0, 7]
    row8 = lax.broadcasted_iota(jnp.int32, (8, 128), 0)
    for side, at in ((0, PAD + NZ - 8), (1, PAD)):
        for j in range(2):
            spare = row8 == (0 if side == 0 else 7)
            line = PAD + NZ - 1 if side == 0 else PAD
            zs[side, 3 * j] = phe[2 + j, at : at + 8, :]
            zs[side, 3 * j + 1] = jnp.where(spare, vt[2, j, NZ - 1 : NZ, :], lame[2 + j, at : at + 8, :])
            zs[side, 3 * j + 2] = jnp.where(spare, pe[j, line : line + 1, :], rese[2 + j, at : at + 8, :])
        zs[side, 6] = own_edge[at : at + 8, :]

    pl.semaphore_wait(barrier, 4)

    def send(src, dst, send_sem, recv_sem, device):
        copy = pltpu.make_async_remote_copy(src, dst, send_sem, recv_sem, device_id=device, device_id_type=MESH)
        copy.start()
        return copy

    to_z = [
        send(zs.at[s], rz.at[s], send_z.at[s], recv_z.at[s], device) for s, device in ((0, z_after), (1, z_before))
    ]
    to_x = [
        send(src, dst, send_x.at[k], recv_x.at[k], device)
        for k, (src, dst, device) in enumerate(
            (
                (ph_hbm.at[1:8], rx_ph.at[0, 1:8], x_after),
                (ph_hbm.at[0:7], rx_ph.at[1, 0:7], x_before),
                (lam.at[2:8], rx_lam.at[0, 2:8], x_after),
                (lam.at[0:6], rx_lam.at[1, 0:6], x_before),
                (edge_out, ne.at[0:2], x_after),
                (edge_out_p0(ps), ne.at[2:3], x_before),
                (res.at[3:8], rx_res.at[0, 3:8], x_after),
                (res.at[0:6], rx_res.at[1, 0:6], x_before),
            )
        )
    ]

    inside_x = (w > 0, w < nw - 1)
    inside_z = (n > 0, n < nn - 1)
    to_d = []
    for s in range(2):
        to_z[s].wait_recv()
        at = PAD - 8 if s == 0 else PAD + NZ
        spare = row8 == (0 if s == 0 else 7)
        line = PAD if s == 0 else PAD + NZ - 1
        own_edge[at : at + 8, :] = rz[s, 6]
        for j in range(2):
            phe[2 + j, at : at + 8, :] = jnp.where(inside_z[s], rz[s, 3 * j], 2.0)
            lame[2 + j, at : at + 8, :] = rz[s, 3 * j + 1]
            rese[2 + j, at : at + 8, :] = rz[s, 3 * j + 2]
            pressure = jnp.where(inside_z[s], rz[s, 3 * j + 2], 0.0)
            if s == 0:
                speed = jnp.where(inside_z[s], rz[s, 3 * j + 1], 0.0)
            else:
                speed = vt[2, j, NZ - 1 : NZ, :]
                pe[j, at : at + 1, :] = pressure[7:8, :]
            rz[s, 3 * j + 1] = jnp.where(spare, speed, rz[s, 3 * j + 1])
            rz[s, 3 * j + 2] = jnp.where(spare, pressure - pe[j, line : line + 1, :], rz[s, 3 * j + 2])
        for k, device in ((0, x_after), (1, x_before)):
            to_d.append(send(rz.at[s], rd.at[k, s], send_d.at[k, s], recv_d.at[k, s], device))

    for k in range(2):
        to_x[k].wait_recv()
        for j in range(2):
            block = turned(rx_ph[k, 4 * j : 4 * j + 4].astype(F32))
            phe[4 * k + j, main, :] = jnp.where(inside_x[k], block, 2.0)

    @pl.loop(0, 14)
    def _(i):
        coefficients(phe, coef, inv, diag, pl.multiple_of(PAD + 8 + 8 * i, 8), 8)

    for k in range(2):
        to_x[2 + k].wait_recv()
        for j in range(2):
            lame[4 * k + j, main, :] = turned(rx_lam[k, 4 * j : 4 * j + 4])
    for k in range(2):
        to_x[4 + k].wait_recv()
    lane128 = lanes(NZ)
    outside = ((lane128 < 64) & jnp.logical_not(inside_x[0])) | (
        (lane128 >= 64) & (lane128 < 96) & jnp.logical_not(inside_x[1])
    )
    near = jnp.where(outside, 0.0, turned(ne[...]))
    near_edge[main, :] = near
    pe[2, main, :] = pltpu.roll(near, 64, 1)
    for k in range(2):
        to_x[6 + k].wait_recv()
        for j in range(2):
            rese[4 * k + j, main, :] = turned(rx_res[k, 4 * j : 4 * j + 4])

    for copy in to_d:
        copy.wait_recv()
    lane = lanes(8)
    for s in range(2):
        at = PAD - 8 if s == 0 else PAD + NZ
        for k in range(2):
            for j in range(2):
                c = 4 * k + j
                phe[c, at : at + 8, :] = jnp.where(jnp.logical_and(inside_x[k], inside_z[s]), rd[k, s, 3 * j], 2.0)
                lame[c, at : at + 8, :] = rd[k, s, 3 * j + 1]
                rese[c, at : at + 8, :] = rd[k, s, 3 * j + 2]
        below = jnp.where(inside_x[0], jnp.where(lane < 32, pltpu.roll(rd[0, s, 6], 64, 1), rd[0, s, 6]), 0.0)
        above = jnp.where(inside_x[1], pltpu.roll(rd[1, s, 6], 64, 1), 0.0)
        near_edge[at : at + 8, :] = jnp.where(
            lane < 64, below, jnp.where(lane < 96, above, own_edge[at : at + 8, :])
        )
    for r in (PAD - 8, PAD, PAD + NZ - 8, PAD + NZ):
        coefficients(phe, coef, inv, diag, r, 8)

    @pl.loop(0, 18)
    def _(i):
        starts(
            lame, rese, inv, coef, near_edge, own_edge, s5, e0, pl.multiple_of(PAD - 8 + 8 * i, 8), 8
        )

    for s in range(2):
        spare = 0 if s == 0 else 7
        for c in range(6):
            j = c % 2
            rows_from = rz.at[s] if c in (2, 3) else rd.at[0 if c < 2 else 1, s]
            speed = rows_from[3 * j + 1, spare : spare + 1, :]
            step = rows_from[3 * j + 2, spare : spare + 1, :]
            own, other = (PAD, PAD - 1) if s == 0 else (PAD + NZ - 1, PAD + NZ)
            c_own = coef[ZD if s == 0 else ZU, c, own : own + 1, :]
            c_other = coef[ZU if s == 0 else ZD, c, other : other + 1, :]
            sign = -W[5] if s == 0 else W[5]
            s5[c, own : own + 1, :] += sign * (c_own * speed)
            s5[c, other : other + 1, :] -= sign * (c_other * speed)
            e0[c, own : own + 1, :] += W[0] * (c_own * step)
            e0[c, other : other + 1, :] -= W[0] * (c_other * step)
    for copy in to_z + to_x + to_d:
        copy.wait_send()


def edge_out_p0(ps):
    return ps.at[0:1]


def neighbours(src, coef, tiles, have, row, rows):
    lane = lanes(rows)
    cur = {c: src[c, pl.ds(row, rows), :] for c in have}
    out = {}
    for c in tiles:
        v = cur[c]
        near = [
            x_up(v, cur.get(c + 1), lane),
            x_down(v, cur.get(c - 1), lane),
            y_up(v),
            y_down(v),
            src[c, pl.ds(row + 1, rows), :],
            src[c, pl.ds(row - 1, rows), :],
        ]
        prod = [coef[k, c, pl.ds(row, rows), :] * near[k] for k in range(6)]
        out[c] = (v, (prod[0] + prod[1]) + (prod[2] + prod[3]) + (prod[4] + prod[5]))
    return out


def chains(coef, s5, e0, pe, diag, vt, gd, gp, gf, s, e, rr, out):
    step = 8

    def sweep(src, dst, tiles, have, keep, scale, first=PAD - 8, last=PAD + NZ + 8):
        @pl.loop(0, (last - first) // step)
        def _(i):
            row = pl.multiple_of(first + step * i, 8)
            for c, (v, total) in neighbours(src, coef, tiles, have, row, step).items():
                dst[c, pl.ds(row, step), :] = keep * v + scale * total

    ss = [s.at[m] for m in range(5)] + [s5]
    ee = [e0] + [e.at[m] for m in range(5)]
    every, middle = range(6), range(1, 5)
    for m in range(5, 0, -1):
        sweep(ss[m], ss[m - 1], every if m == 5 else middle, every if m >= 4 else middle,
              W[m - 1] / W[m] * (1.0 - W[m]), W[m - 1])
    for m in range(5):
        tiles = (range(1, 6), middle, middle, middle, range(2, 5))[m]
        have = (every, range(1, 6), middle, middle, middle)[m]
        sweep(ee[m], ee[m + 1], tiles, have, W[m + 1] / W[m] * (1.0 - W[m]), W[m + 1])

    @pl.loop(0, 17)
    def _(i):
        row = pl.multiple_of(PAD + 8 * i, 8)
        for c in range(2, 5):
            total = None
            for m in range(6):
                term = ss[m][c, pl.ds(row, 8), :] * ee[m][c, pl.ds(row, 8), :] * (1.0 / W[m])
                total = term if total is None else total + term
            rr[c - 2, pl.ds(row, 8), :] = total

    @pl.loop(0, 16)
    def _(i):
        row = pl.multiple_of(PAD + 8 * i, 8)
        own = pl.multiple_of(8 * i, 8)
        lane = lanes(8)
        last = (lane & 31) == 31

        def rises(ref, c, at):
            v = ref[at, pl.ds(row, 8), :]
            after = ref[at + 1, pl.ds(row, 8), :]
            return v, (
                x_up(v, after, lane),
                jnp.where(last, 0.0, y_up(v)),
                ref[at, pl.ds(row + 1, 8), :],
            )

        for j in range(2):
            c = 2 + j
            p, up = rises(pe, c, j)
            rise = [p - u for u in up]
            grads = [None] * 3
            total = None
            for m in range(6):
                v, up = rises(ss[m], c, c)
                for a in range(3):
                    term = (v - up[a]) * rise[a]
                    grads[a] = term if grads[a] is None else grads[a] + term
                total = v if total is None else total + v
                v, up = rises(ee[m], c, c)
                rise = [r + (v - u) for r, u in zip(rise, up)]
            v, up = rises(rr, c, j)
            out[0, j, pl.ds(own, 8), :] = total
            for a in range(3):
                out[2 + a, j, pl.ds(own, 8), :] = (
                    vt[a, j, pl.ds(own, 8), :] * rise[a] - grads[a] - (v + up[a])
                )
        for c, (v, total) in neighbours(ss[0], coef, (2, 3), middle, row, 8).items():
            out[1, c - 2, pl.ds(own, 8), :] = diag[c - 2, pl.ds(row, 8), :] * (
                (1.0 / W[0] - 1.0) * v + total
            )

    for j in range(2):
        part = slice(4 * j, 4 * j + 4)
        gd[part] = jnp.transpose(out[0, j]).reshape(4, NY, NZ)
        gp[part] = jnp.transpose(out[1, j]).reshape(4, NY, NZ)
        for a in range(3):
            gf[a, part] = jnp.transpose(out[2 + a, j]).reshape(4, NY, NZ)


def per_device(divergence, pressure_start, phase, velocity_cot):
    shape = jax.ShapeDtypeStruct
    vmem = pl.BlockSpec(memory_space=pltpu.VMEM)
    dma = pltpu.SemaphoreType.DMA
    args = [
        pltpu.with_memory_space_constraint(a, pltpu.HBM)
        for a in (divergence, pressure_start, phase, velocity_cot)
    ]
    block, tiles = (8, NY, NZ), (6, ROWS, 128)
    made = pl.pallas_call(
        exchange,
        out_shape=[
            shape((6, *tiles), F32),
            shape(tiles, F32),
            shape(tiles, F32),
            shape((3, ROWS, 128), F32),
            shape((2, ROWS, 128), F32),
            shape((3, 2, NZ, 128), F32),
        ],
        in_specs=[pl.BlockSpec(memory_space=pltpu.HBM)] * 4,
        out_specs=[vmem] * 6,
        scratch_shapes=[
            pltpu.VMEM(block, jnp.int32),
            pltpu.VMEM(block, F32),
            pltpu.VMEM(block, F32),
            pltpu.VMEM((3, *block), F32),
            pltpu.VMEM(block, F32),
            pltpu.VMEM(block, F32),
            pltpu.VMEM((2, *block), jnp.int32),
            pltpu.VMEM((2, *block), F32),
            pltpu.VMEM((2, *block), F32),
            pltpu.VMEM((4, NY, NZ), F32),
            pltpu.VMEM((2, NY, NZ), F32),
            pltpu.VMEM((2, 7, 8, 128), F32),
            pltpu.VMEM((2, 7, 8, 128), F32),
            pltpu.VMEM((2, 2, 7, 8, 128), F32),
            pltpu.VMEM(tiles, F32),
            pltpu.VMEM(tiles, F32),
            pltpu.VMEM(tiles, F32),
            pltpu.VMEM(tiles, F32),
            pltpu.VMEM((ROWS, 128), F32),
            pltpu.VMEM((ROWS, 128), F32),
            dma((4,)),
            dma((8,)),
            dma((8,)),
            dma((2,)),
            dma((2,)),
            dma((2, 2)),
            dma((2, 2)),
        ],
        compiler_params=pltpu.CompilerParams(
            collective_id=0, has_side_effects=True, vmem_limit_bytes=24 << 20
        ),
        name="exchange",
    )(*args)
    return tuple(
        pl.pallas_call(
            chains,
            out_shape=[shape(block, F32), shape(block, F32), shape((3, *block), F32)],
            in_specs=[vmem] * 6,
            out_specs=[vmem] * 3,
            scratch_shapes=[
                pltpu.VMEM((5, *tiles), F32),
                pltpu.VMEM((5, *tiles), F32),
                pltpu.VMEM((3, ROWS, 128), F32),
                pltpu.VMEM((5, 2, NZ, 128), F32),
            ],
            compiler_params=pltpu.CompilerParams(vmem_limit_bytes=24 << 20),
            name="chains",
        )(*made)
    )


def solution(mesh):
    field = P("wide", None, "narrow")
    faces = P(None, "wide", None, "narrow")
    return jax.shard_map(
        per_device,
        mesh=mesh,
        in_specs=(field, field, field, faces),
        out_specs=(field, field, faces),
        check_vma=False,
    )
```

```python
import math

import jax
import jax.numpy as jnp
from jax import lax
from jax.experimental import pallas as pl
from jax.experimental.pallas import tpu as pltpu
from jax.sharding import PartitionSpec as P

SWEEPS = 6
CENTER, RADIUS = 1.125, 0.875
PAD = 16
ROWS = 160
NZ = 128
NY = 32
F32 = jnp.float32
MESH = pl.DeviceIdType.MESH
XU, XD, YU, YD, ZU, ZD = range(6)


def chebyshev_weights():
    roots = [CENTER + RADIUS * math.cos(math.pi * (2 * m + 1) / (2 * SWEEPS)) for m in range(SWEEPS)]
    order = []
    for m in range(SWEEPS // 2):
        order += [m, SWEEPS - 1 - m]
    return [1.0 / roots[m] for m in order]


W = chebyshev_weights()


def lanes(rows):
    return lax.broadcasted_iota(jnp.int32, (rows, 128), 1)


def x_up(tile, after, lane):
    return pltpu.roll(tile if after is None else jnp.where(lane < 32, after, tile), 96, 1)


def x_down(tile, before, lane):
    return pltpu.roll(tile if before is None else jnp.where(lane >= 96, before, tile), 32, 1)


def y_up(tile):
    return pltpu.roll(tile, 127, 1)


def y_down(tile):
    return pltpu.roll(tile, 1, 1)


def turned(block):
    return jnp.transpose(block.reshape(128, 128))


def local_sums(ph, ps, dv, vc, lam, res):
    row = lax.broadcasted_iota(jnp.int32, (NY, NZ), 0)
    lane = lax.broadcasted_iota(jnp.int32, (NY, NZ), 1)
    top, bottom, inner = row == NY - 1, row == 0, lane < NZ - 1
    before_lam = before_res = None
    here = ph[0].astype(F32)
    for x in range(8):
        a = here
        base, slope = 1.0 + 0.6 * a, 0.6 + 1.8 * a
        p = ps[x]
        face_y = base + slope * jnp.where(top, a, pltpu.roll(a, NY - 1, 0))
        face_z = jnp.where(inner, base + slope * pltpu.roll(a, NZ - 1, 1), 0.0)
        flux_y = face_y * vc[1, x]
        flux_z = face_z * vc[2, x]
        flow_y = face_y * (p - jnp.where(top, 0.0, pltpu.roll(p, NY - 1, 0)))
        flow_z = face_z * (p - pltpu.roll(p, NZ - 1, 1))
        total = flux_y - jnp.where(bottom, 0.0, pltpu.roll(flux_y, 1, 0)) + flux_z - pltpu.roll(flux_z, 1, 1)
        lower = jnp.where(bottom, -(1.0 + 3.0 * a) * p, pltpu.roll(flow_y, 1, 0))
        rest = dv[x] - (flow_y - lower) - (flow_z - pltpu.roll(flow_z, 1, 1))
        if x > 0:
            total = total - before_lam
            rest = rest + before_res
        if x < 7:
            here = ph[x + 1].astype(F32)
            face_x = base + slope * here
            before_lam = face_x * vc[0, x]
            before_res = face_x * (p - ps[x + 1])
            total = total + before_lam
            rest = rest - before_res
        lam[x] = total
        res[x] = rest


def coefficients(phe, coef, inv, diag, row, rows):
    lane = lanes(rows)
    last, first = (lane & 31) == 31, (lane & 31) == 0
    cur = [phe[c, pl.ds(row, rows), :] for c in range(6)]
    for c in range(6):
        a = cur[c]
        near = [
            x_up(a, cur[c + 1] if c < 5 else None, lane),
            x_down(a, cur[c - 1] if c > 0 else None, lane),
            jnp.where(last, a, y_up(a)),
            jnp.where(first, a, y_down(a)),
            phe[c, pl.ds(row + 1, rows), :],
            phe[c, pl.ds(row - 1, rows), :],
        ]
        near = [b if k in (YU, YD) else jnp.where(b > 1.5, a, b) for k, b in enumerate(near)]
        base, slope = 1.0 + 0.6 * a, 0.6 + 1.8 * a
        total = 6.0 * base + slope * ((near[0] + near[1]) + (near[2] + near[3]) + (near[4] + near[5]))
        inverse = jnp.where(a > 1.5, 0.0, 1.0 / total)
        inv[c, pl.ds(row, rows), :] = inverse
        base, slope = base * inverse, slope * inverse
        for k in range(6):
            value = base + slope * near[k]
            if k == YU:
                value = jnp.where(last, 0.0, value)
            if k == YD:
                value = jnp.where(first, 0.0, value)
            coef[k, c, pl.ds(row, rows), :] = value
        if c in (2, 3):
            diag[c - 2, pl.ds(row, rows), :] = total


def starts(lame, rese, inv, coef, near_edge, own_edge, s5, e0, row, rows):
    lane = lanes(rows)
    low, high = lane < 32, lane >= 96
    ne = near_edge[pl.ds(row, rows), :]
    step = ne - own_edge[pl.ds(row, rows), :]
    for c in range(6):
        i = inv[c, pl.ds(row, rows), :]
        lam = i * lame[c, pl.ds(row, rows), :]
        res = i * rese[c, pl.ds(row, rows), :]
        if c == 1:
            cf = coef[XU, c, pl.ds(row, rows), :]
            lam = lam + jnp.where(high, cf * pltpu.roll(ne, 64, 1), 0.0)
            res = res - jnp.where(high, cf * pltpu.roll(step, 96, 1), 0.0)
        elif c == 2:
            cf = coef[XD, c, pl.ds(row, rows), :]
            lam = lam - jnp.where(low, cf * pltpu.roll(ne, 96, 1), 0.0)
            res = res + jnp.where(low, cf * step, 0.0)
        elif c == 3:
            cf = coef[XU, c, pl.ds(row, rows), :]
            lam = lam + jnp.where(high, cf * ne, 0.0)
            res = res + jnp.where(high, cf * pltpu.roll(step, 32, 1), 0.0)
        elif c == 4:
            cf = coef[XD, c, pl.ds(row, rows), :]
            lam = lam - jnp.where(low, cf * pltpu.roll(ne, 32, 1), 0.0)
            res = res - jnp.where(low, cf * pltpu.roll(step, 64, 1), 0.0)
        s5[c, pl.ds(row, rows), :] = W[5] * lam
        e0[c, pl.ds(row, rows), :] = W[0] * res


def exchange(
    dv_hbm, ps_hbm, ph_hbm, vc_hbm,
    coef, s5, e0, pe, diag, vt,
    ph, ps, dv, vc, lam, res, rx_ph, rx_lam, rx_res, ne, edge_out, zs, rz, rd,
    phe, lame, rese, inv, near_edge, own_edge,
    in_sem, send_x, recv_x, send_z, recv_z, send_d, recv_d,
):
    w, n = lax.axis_index("wide"), lax.axis_index("narrow")
    nw, nn = lax.axis_size("wide"), lax.axis_size("narrow")
    x_after, x_before = (lax.rem(w + 1, nw), n), (lax.rem(w + nw - 1, nw), n)
    z_after, z_before = (w, lax.rem(n + 1, nn)), (w, lax.rem(n + nn - 1, nn))
    barrier = pltpu.get_barrier_semaphore()
    for device in (x_after, x_before, z_after, z_before):
        pl.semaphore_signal(barrier, inc=1, device_id=device, device_id_type=MESH)
    loads = [
        pltpu.make_async_copy(src, dst, in_sem.at[k])
        for k, (src, dst) in enumerate(((ph_hbm, ph), (ps_hbm, ps), (dv_hbm, dv), (vc_hbm, vc)))
    ]
    for load in loads:
        load.start()
    zero = jnp.zeros((NY, NZ), F32)
    rx_ph[0, 0] = jnp.zeros((NY, NZ), jnp.int32)
    rx_ph[1, 7] = jnp.zeros((NY, NZ), jnp.int32)
    for k in (0, 1):
        rx_lam[0, k] = zero
        rx_res[0, k] = zero
        rx_lam[1, 6 + k] = zero
        rx_res[1, 6 + k] = zero
    rx_res[0, 2] = zero
    for c in range(6):
        for r in (0, 152):
            phe[c, r : r + 8, :] = jnp.zeros((8, 128), F32)
            s5[c, r : r + 8, :] = jnp.zeros((8, 128), F32)
            e0[c, r : r + 8, :] = jnp.zeros((8, 128), F32)
    for load in loads:
        load.wait()

    local_sums(ph, ps, dv, vc, lam, res)
    main = slice(PAD, PAD + NZ)
    for j in range(2):
        part = slice(4 * j, 4 * j + 4)
        phe[2 + j, main, :] = turned(ph[part].astype(F32))
        lame[2 + j, main, :] = turned(lam[part])
        rese[2 + j, main, :] = turned(res[part])
        pe[j, main, :] = turned(ps[part])
        for a in range(3):
            vt[a, j] = turned(vc[a, part])
    own_edge[main, :] = turned(jnp.stack([ps[0], vc[0, 7], ps[7], vc[0, 7]]))
    edge_out[0] = ps[7]
    edge_out[1] = vc[0, 7]
    ne[3] = vc[0, 7]
    row8 = lax.broadcasted_iota(jnp.int32, (8, 128), 0)
    for side, at in ((0, PAD + NZ - 8), (1, PAD)):
        for j in range(2):
            spare = row8 == (0 if side == 0 else 7)
            line = PAD + NZ - 1 if side == 0 else PAD
            zs[side, 3 * j] = phe[2 + j, at : at + 8, :]
            zs[side, 3 * j + 1] = jnp.where(spare, vt[2, j, NZ - 1 : NZ, :], lame[2 + j, at : at + 8, :])
            zs[side, 3 * j + 2] = jnp.where(spare, pe[j, line : line + 1, :], rese[2 + j, at : at + 8, :])
        zs[side, 6] = own_edge[at : at + 8, :]

    pl.semaphore_wait(barrier, 4)

    def send(src, dst, send_sem, recv_sem, device):
        copy = pltpu.make_async_remote_copy(src, dst, send_sem, recv_sem, device_id=device, device_id_type=MESH)
        copy.start()
        return copy

    to_z = [
        send(zs.at[s], rz.at[s], send_z.at[s], recv_z.at[s], device) for s, device in ((0, z_after), (1, z_before))
    ]
    to_x = [
        send(src, dst, send_x.at[k], recv_x.at[k], device)
        for k, (src, dst, device) in enumerate(
            (
                (ph_hbm.at[1:8], rx_ph.at[0, 1:8], x_after),
                (ph_hbm.at[0:7], rx_ph.at[1, 0:7], x_before),
                (lam.at[2:8], rx_lam.at[0, 2:8], x_after),
                (lam.at[0:6], rx_lam.at[1, 0:6], x_before),
                (edge_out, ne.at[0:2], x_after),
                (edge_out_p0(ps), ne.at[2:3], x_before),
                (res.at[3:8], rx_res.at[0, 3:8], x_after),
                (res.at[0:6], rx_res.at[1, 0:6], x_before),
            )
        )
    ]

    inside_x = (w > 0, w < nw - 1)
    inside_z = (n > 0, n < nn - 1)
    to_d = []
    for s in range(2):
        to_z[s].wait_recv()
        at = PAD - 8 if s == 0 else PAD + NZ
        spare = row8 == (0 if s == 0 else 7)
        line = PAD if s == 0 else PAD + NZ - 1
        own_edge[at : at + 8, :] = rz[s, 6]
        for j in range(2):
            phe[2 + j, at : at + 8, :] = jnp.where(inside_z[s], rz[s, 3 * j], 2.0)
            lame[2 + j, at : at + 8, :] = rz[s, 3 * j + 1]
            rese[2 + j, at : at + 8, :] = rz[s, 3 * j + 2]
            pressure = jnp.where(inside_z[s], rz[s, 3 * j + 2], 0.0)
            if s == 0:
                speed = jnp.where(inside_z[s], rz[s, 3 * j + 1], 0.0)
            else:
                speed = vt[2, j, NZ - 1 : NZ, :]
                pe[j, at : at + 1, :] = pressure[7:8, :]
            rz[s, 3 * j + 1] = jnp.where(spare, speed, rz[s, 3 * j + 1])
            rz[s, 3 * j + 2] = jnp.where(spare, pressure - pe[j, line : line + 1, :], rz[s, 3 * j + 2])
        for k, device in ((0, x_after), (1, x_before)):
            to_d.append(send(rz.at[s], rd.at[k, s], send_d.at[k, s], recv_d.at[k, s], device))

    for k in range(2):
        to_x[k].wait_recv()
        for j in range(2):
            block = turned(rx_ph[k, 4 * j : 4 * j + 4].astype(F32))
            phe[4 * k + j, main, :] = jnp.where(inside_x[k], block, 2.0)

    for row in range(PAD + 8, PAD + NZ - 8, 16):
        coefficients(phe, coef, inv, diag, row, 16)

    for k in range(2):
        to_x[2 + k].wait_recv()
        for j in range(2):
            lame[4 * k + j, main, :] = turned(rx_lam[k, 4 * j : 4 * j + 4])
    for k in range(2):
        to_x[4 + k].wait_recv()
    lane128 = lanes(NZ)
    outside = ((lane128 < 64) & jnp.logical_not(inside_x[0])) | (
        (lane128 >= 64) & (lane128 < 96) & jnp.logical_not(inside_x[1])
    )
    near = jnp.where(outside, 0.0, turned(ne[...]))
    near_edge[main, :] = near
    pe[2, main, :] = pltpu.roll(near, 64, 1)
    for k in range(2):
        to_x[6 + k].wait_recv()
        for j in range(2):
            rese[4 * k + j, main, :] = turned(rx_res[k, 4 * j : 4 * j + 4])

    for copy in to_d:
        copy.wait_recv()
    lane = lanes(8)
    for s in range(2):
        at = PAD - 8 if s == 0 else PAD + NZ
        for k in range(2):
            for j in range(2):
                c = 4 * k + j
                phe[c, at : at + 8, :] = jnp.where(jnp.logical_and(inside_x[k], inside_z[s]), rd[k, s, 3 * j], 2.0)
                lame[c, at : at + 8, :] = rd[k, s, 3 * j + 1]
                rese[c, at : at + 8, :] = rd[k, s, 3 * j + 2]
        below = jnp.where(inside_x[0], jnp.where(lane < 32, pltpu.roll(rd[0, s, 6], 64, 1), rd[0, s, 6]), 0.0)
        above = jnp.where(inside_x[1], pltpu.roll(rd[1, s, 6], 64, 1), 0.0)
        near_edge[at : at + 8, :] = jnp.where(
            lane < 64, below, jnp.where(lane < 96, above, own_edge[at : at + 8, :])
        )
    for r in (PAD - 8, PAD, PAD + NZ - 8, PAD + NZ):
        coefficients(phe, coef, inv, diag, r, 8)

    for row in range(PAD - 8, PAD + NZ + 8, 24):
        starts(lame, rese, inv, coef, near_edge, own_edge, s5, e0, row, 24)

    for s in range(2):
        spare = 0 if s == 0 else 7
        for c in range(6):
            j = c % 2
            rows_from = rz.at[s] if c in (2, 3) else rd.at[0 if c < 2 else 1, s]
            speed = rows_from[3 * j + 1, spare : spare + 1, :]
            step = rows_from[3 * j + 2, spare : spare + 1, :]
            own, other = (PAD, PAD - 1) if s == 0 else (PAD + NZ - 1, PAD + NZ)
            c_own = coef[ZD if s == 0 else ZU, c, own : own + 1, :]
            c_other = coef[ZU if s == 0 else ZD, c, other : other + 1, :]
            sign = -W[5] if s == 0 else W[5]
            s5[c, own : own + 1, :] += sign * (c_own * speed)
            s5[c, other : other + 1, :] -= sign * (c_other * speed)
            e0[c, own : own + 1, :] += W[0] * (c_own * step)
            e0[c, other : other + 1, :] -= W[0] * (c_other * step)
    for copy in to_z + to_x + to_d:
        copy.wait_send()


def edge_out_p0(ps):
    return ps.at[0:1]


def neighbours(src, coef, tiles, have, row, rows):
    lane = lanes(rows)
    cur = {c: src[c, pl.ds(row, rows), :] for c in have}
    out = {}
    for c in tiles:
        v = cur[c]
        near = [
            x_up(v, cur.get(c + 1), lane),
            x_down(v, cur.get(c - 1), lane),
            y_up(v),
            y_down(v),
            src[c, pl.ds(row + 1, rows), :],
            src[c, pl.ds(row - 1, rows), :],
        ]
        prod = [coef[k, c, pl.ds(row, rows), :] * near[k] for k in range(6)]
        out[c] = (v, (prod[0] + prod[1]) + (prod[2] + prod[3]) + (prod[4] + prod[5]))
    return out


def chains(coef, s5, e0, pe, diag, vt, gd, gp, gf, s, e, rr, out):
    step = 24

    def sweep(src, dst, tiles, have, keep, scale, first=PAD - 8, last=PAD + NZ + 8):
        for row in range(first, last, step):
            for c, (v, total) in neighbours(src, coef, tiles, have, row, step).items():
                dst[c, pl.ds(row, step), :] = keep * v + scale * total

    ss = [s.at[m] for m in range(5)] + [s5]
    ee = [e0] + [e.at[m] for m in range(5)]
    every, middle = range(6), range(1, 5)
    for m in range(5, 0, -1):
        sweep(ss[m], ss[m - 1], every if m == 5 else middle, every if m >= 4 else middle,
              W[m - 1] / W[m] * (1.0 - W[m]), W[m - 1])
    for m in range(5):
        tiles = (range(1, 6), middle, middle, middle, range(2, 5))[m]
        have = (every, range(1, 6), middle, middle, middle)[m]
        sweep(ee[m], ee[m + 1], tiles, have, W[m + 1] / W[m] * (1.0 - W[m]), W[m + 1])

    for row in (PAD,):
        for c in range(2, 5):
            total = None
            for m in range(6):
                term = ss[m][c, pl.ds(row, 136), :] * ee[m][c, pl.ds(row, 136), :] * (1.0 / W[m])
                total = term if total is None else total + term
            rr[c - 2, pl.ds(row, 136), :] = total

    for i in range(16):
        row = PAD + 8 * i
        own = 8 * i
        lane = lanes(8)
        last = (lane & 31) == 31

        def rises(ref, c, at):
            v = ref[at, pl.ds(row, 8), :]
            after = ref[at + 1, pl.ds(row, 8), :]
            return v, (
                x_up(v, after, lane),
                jnp.where(last, 0.0, y_up(v)),
                ref[at, pl.ds(row + 1, 8), :],
            )

        for j in range(2):
            c = 2 + j
            p, up = rises(pe, c, j)
            rise = [p - u for u in up]
            grads = [None] * 3
            total = None
            for m in range(6):
                v, up = rises(ss[m], c, c)
                for a in range(3):
                    term = (v - up[a]) * rise[a]
                    grads[a] = term if grads[a] is None else grads[a] + term
                total = v if total is None else total + v
                v, up = rises(ee[m], c, c)
                rise = [r + (v - u) for r, u in zip(rise, up)]
            v, up = rises(rr, c, j)
            out[0, j, pl.ds(own, 8), :] = total
            for a in range(3):
                out[2 + a, j, pl.ds(own, 8), :] = (
                    vt[a, j, pl.ds(own, 8), :] * rise[a] - grads[a] - (v + up[a])
                )
        for c, (v, total) in neighbours(ss[0], coef, (2, 3), middle, row, 8).items():
            out[1, c - 2, pl.ds(own, 8), :] = diag[c - 2, pl.ds(row, 8), :] * (
                (1.0 / W[0] - 1.0) * v + total
            )

    for j in range(2):
        part = slice(4 * j, 4 * j + 4)
        gd[part] = jnp.transpose(out[0, j]).reshape(4, NY, NZ)
        gp[part] = jnp.transpose(out[1, j]).reshape(4, NY, NZ)
        for a in range(3):
            gf[a, part] = jnp.transpose(out[2 + a, j]).reshape(4, NY, NZ)


def per_device(divergence, pressure_start, phase, velocity_cot):
    shape = jax.ShapeDtypeStruct
    vmem = pl.BlockSpec(memory_space=pltpu.VMEM)
    dma = pltpu.SemaphoreType.DMA
    args = [
        pltpu.with_memory_space_constraint(a, pltpu.HBM)
        for a in (divergence, pressure_start, phase, velocity_cot)
    ]
    block, tiles = (8, NY, NZ), (6, ROWS, 128)
    made = pl.pallas_call(
        exchange,
        out_shape=[
            shape((6, *tiles), F32),
            shape(tiles, F32),
            shape(tiles, F32),
            shape((3, ROWS, 128), F32),
            shape((2, ROWS, 128), F32),
            shape((3, 2, NZ, 128), F32),
        ],
        in_specs=[pl.BlockSpec(memory_space=pltpu.HBM)] * 4,
        out_specs=[vmem] * 6,
        scratch_shapes=[
            pltpu.VMEM(block, jnp.int32),
            pltpu.VMEM(block, F32),
            pltpu.VMEM(block, F32),
            pltpu.VMEM((3, *block), F32),
            pltpu.VMEM(block, F32),
            pltpu.VMEM(block, F32),
            pltpu.VMEM((2, *block), jnp.int32),
            pltpu.VMEM((2, *block), F32),
            pltpu.VMEM((2, *block), F32),
            pltpu.VMEM((4, NY, NZ), F32),
            pltpu.VMEM((2, NY, NZ), F32),
            pltpu.VMEM((2, 7, 8, 128), F32),
            pltpu.VMEM((2, 7, 8, 128), F32),
            pltpu.VMEM((2, 2, 7, 8, 128), F32),
            pltpu.VMEM(tiles, F32),
            pltpu.VMEM(tiles, F32),
            pltpu.VMEM(tiles, F32),
            pltpu.VMEM(tiles, F32),
            pltpu.VMEM((ROWS, 128), F32),
            pltpu.VMEM((ROWS, 128), F32),
            dma((4,)),
            dma((8,)),
            dma((8,)),
            dma((2,)),
            dma((2,)),
            dma((2, 2)),
            dma((2, 2)),
        ],
        compiler_params=pltpu.CompilerParams(
            collective_id=0, has_side_effects=True, vmem_limit_bytes=24 << 20
        ),
        name="exchange",
    )(*args)
    return tuple(
        pl.pallas_call(
            chains,
            out_shape=[shape(block, F32), shape(block, F32), shape((3, *block), F32)],
            in_specs=[vmem] * 6,
            out_specs=[vmem] * 3,
            scratch_shapes=[
                pltpu.VMEM((5, *tiles), F32),
                pltpu.VMEM((5, *tiles), F32),
                pltpu.VMEM((3, ROWS, 128), F32),
                pltpu.VMEM((5, 2, NZ, 128), F32),
            ],
            compiler_params=pltpu.CompilerParams(vmem_limit_bytes=24 << 20),
            name="chains",
        )(*made)
    )


def solution(mesh):
    field = P("wide", None, "narrow")
    faces = P(None, "wide", None, "narrow")
    return jax.shard_map(
        per_device,
        mesh=mesh,
        in_specs=(field, field, field, faces),
        out_specs=(field, field, faces),
        check_vma=False,
    )
```

```python
import math

import jax
import jax.numpy as jnp
from jax import lax
from jax.experimental import pallas as pl
from jax.experimental.pallas import tpu as pltpu
from jax.sharding import PartitionSpec as P

SWEEPS = 6
CENTER, RADIUS = 1.125, 0.875
PAD = 16
ROWS = 160
NZ = 128
NY = 32
F32 = jnp.float32
MESH = pl.DeviceIdType.MESH
XU, XD, YU, YD, ZU, ZD = range(6)


def chebyshev_weights():
    roots = [CENTER + RADIUS * math.cos(math.pi * (2 * m + 1) / (2 * SWEEPS)) for m in range(SWEEPS)]
    order = []
    for m in range(SWEEPS // 2):
        order += [m, SWEEPS - 1 - m]
    return [1.0 / roots[m] for m in order]


W = chebyshev_weights()


def lanes(rows):
    return lax.broadcasted_iota(jnp.int32, (rows, 128), 1)


def x_up(tile, after, lane):
    return pltpu.roll(tile if after is None else jnp.where(lane < 32, after, tile), 96, 1)


def x_down(tile, before, lane):
    return pltpu.roll(tile if before is None else jnp.where(lane >= 96, before, tile), 32, 1)


def y_up(tile):
    return pltpu.roll(tile, 127, 1)


def y_down(tile):
    return pltpu.roll(tile, 1, 1)


def turned(block):
    return jnp.transpose(block.reshape(128, 128))


def local_sums(ph, ps, dv, vc, lam, res):
    row = lax.broadcasted_iota(jnp.int32, (NY, NZ), 0)
    lane = lax.broadcasted_iota(jnp.int32, (NY, NZ), 1)
    top, bottom, inner = row == NY - 1, row == 0, lane < NZ - 1
    before_lam = before_res = None
    here = ph[0].astype(F32)
    for x in range(8):
        a = here
        base, slope = 1.0 + 0.6 * a, 0.6 + 1.8 * a
        p = ps[x]
        face_y = base + slope * jnp.where(top, a, pltpu.roll(a, NY - 1, 0))
        face_z = jnp.where(inner, base + slope * pltpu.roll(a, NZ - 1, 1), 0.0)
        flux_y = face_y * vc[1, x]
        flux_z = face_z * vc[2, x]
        flow_y = face_y * (p - jnp.where(top, 0.0, pltpu.roll(p, NY - 1, 0)))
        flow_z = face_z * (p - pltpu.roll(p, NZ - 1, 1))
        total = flux_y - jnp.where(bottom, 0.0, pltpu.roll(flux_y, 1, 0)) + flux_z - pltpu.roll(flux_z, 1, 1)
        lower = jnp.where(bottom, -(1.0 + 3.0 * a) * p, pltpu.roll(flow_y, 1, 0))
        rest = dv[x] - (flow_y - lower) - (flow_z - pltpu.roll(flow_z, 1, 1))
        if x > 0:
            total = total - before_lam
            rest = rest + before_res
        if x < 7:
            here = ph[x + 1].astype(F32)
            face_x = base + slope * here
            before_lam = face_x * vc[0, x]
            before_res = face_x * (p - ps[x + 1])
            total = total + before_lam
            rest = rest - before_res
        lam[x] = total
        res[x] = rest


def coefficients(phe, coef, inv, diag, row, rows):
    lane = lanes(rows)
    last, first = (lane & 31) == 31, (lane & 31) == 0
    cur = [phe[c, pl.ds(row, rows), :] for c in range(6)]
    for c in range(6):
        a = cur[c]
        near = [
            x_up(a, cur[c + 1] if c < 5 else None, lane),
            x_down(a, cur[c - 1] if c > 0 else None, lane),
            jnp.where(last, a, y_up(a)),
            jnp.where(first, a, y_down(a)),
            phe[c, pl.ds(row + 1, rows), :],
            phe[c, pl.ds(row - 1, rows), :],
        ]
        near = [b if k in (YU, YD) else jnp.where(b > 1.5, a, b) for k, b in enumerate(near)]
        base, slope = 1.0 + 0.6 * a, 0.6 + 1.8 * a
        total = 6.0 * base + slope * ((near[0] + near[1]) + (near[2] + near[3]) + (near[4] + near[5]))
        inverse = jnp.where(a > 1.5, 0.0, 1.0 / total)
        inv[c, pl.ds(row, rows), :] = inverse
        base, slope = base * inverse, slope * inverse
        for k in range(6):
            value = base + slope * near[k]
            if k == YU:
                value = jnp.where(last, 0.0, value)
            if k == YD:
                value = jnp.where(first, 0.0, value)
            coef[k, c, pl.ds(row, rows), :] = value
        if c in (2, 3):
            diag[c - 2, pl.ds(row, rows), :] = total


def start(right, inv, coef, near_edge, own_edge, dst, scale, residual, row, rows):
    lane = lanes(rows)
    low, high = lane < 32, lane >= 96
    near = near_edge[pl.ds(row, rows), :]
    if residual:
        near = own_edge[pl.ds(row, rows), :] - near
    shifts = (96, 0, 32, 64) if residual else (64, 96, 0, 32)
    for c in range(6):
        value = inv[c, pl.ds(row, rows), :] * right[c, pl.ds(row, rows), :]
        if 1 <= c <= 4:
            face = coef[XU if c in (1, 3) else XD, c, pl.ds(row, rows), :]
            edge = face * (pltpu.roll(near, shifts[c - 1], 1) if shifts[c - 1] else near)
            edge = jnp.where(high if c in (1, 3) else low, edge, 0.0)
            plus = c in (1, 3) if not residual else c in (1, 4)
            value = value + edge if plus else value - edge
        dst[c, pl.ds(row, rows), :] = scale * value


def exchange(
    dv_hbm, ps_hbm, ph_hbm, vc_hbm,
    coef, ss, ee, s_up, e_up, pe, diag, vt,
    ph, ps, dv, vc, lam, res, rx_ph, rx_lam, rx_res, ne, edge_out, zs, rz, rd,
    phe, lame, rese, inv, near_edge, own_edge,
    in_sem, send_x, recv_x, send_z, recv_z, send_d, recv_d,
):
    w, n = lax.axis_index("wide"), lax.axis_index("narrow")
    nw, nn = lax.axis_size("wide"), lax.axis_size("narrow")
    x_after, x_before = (lax.rem(w + 1, nw), n), (lax.rem(w + nw - 1, nw), n)
    z_after, z_before = (w, lax.rem(n + 1, nn)), (w, lax.rem(n + nn - 1, nn))
    s5, e0 = ss.at[5], ee.at[0]
    barrier = pltpu.get_barrier_semaphore()
    for device in (x_after, x_before, z_after, z_before):
        pl.semaphore_signal(barrier, inc=1, device_id=device, device_id_type=MESH)
    loads = [
        pltpu.make_async_copy(src, dst, in_sem.at[k])
        for k, (src, dst) in enumerate(((ph_hbm, ph), (ps_hbm, ps), (dv_hbm, dv), (vc_hbm, vc)))
    ]
    for load in loads:
        load.start()
    zero = jnp.zeros((NY, NZ), F32)
    rx_ph[0, 0] = jnp.zeros((NY, NZ), jnp.int32)
    rx_ph[1, 7] = jnp.zeros((NY, NZ), jnp.int32)
    for k in (0, 1):
        rx_lam[0, k] = zero
        rx_res[0, k] = zero
        rx_lam[1, 6 + k] = zero
        rx_res[1, 6 + k] = zero
    rx_res[0, 2] = zero
    for c in range(6):
        for r in (0, PAD + NZ):
            phe[c, r : r + PAD, :] = jnp.zeros((PAD, 128), F32)
            ss[5, c, r : r + PAD, :] = jnp.zeros((PAD, 128), F32)
            ee[0, c, r : r + PAD, :] = jnp.zeros((PAD, 128), F32)
    for load in loads:
        load.wait()

    local_sums(ph, ps, dv, vc, lam, res)
    main = slice(PAD, PAD + NZ)
    for j in range(2):
        part = slice(4 * j, 4 * j + 4)
        phe[2 + j, main, :] = turned(ph[part].astype(F32))
        lame[2 + j, main, :] = turned(lam[part])
        rese[2 + j, main, :] = turned(res[part])
        pe[j, main, :] = turned(ps[part])
        for a in range(3):
            vt[a, j] = turned(vc[a, part])
    own_edge[main, :] = turned(jnp.stack([ps[0], vc[0, 7], ps[7], vc[0, 7]]))
    edge_out[0] = ps[7]
    edge_out[1] = vc[0, 7]
    ne[3] = vc[0, 7]
    row8 = lax.broadcasted_iota(jnp.int32, (8, 128), 0)
    for side, at in ((0, PAD + NZ - 8), (1, PAD)):
        for j in range(2):
            spare = row8 == (0 if side == 0 else 7)
            line = PAD + NZ - 1 if side == 0 else PAD
            zs[side, 3 * j] = phe[2 + j, at : at + 8, :]
            zs[side, 3 * j + 1] = jnp.where(spare, vt[2, j, NZ - 1 : NZ, :], lame[2 + j, at : at + 8, :])
            zs[side, 3 * j + 2] = jnp.where(spare, pe[j, line : line + 1, :], rese[2 + j, at : at + 8, :])
        zs[side, 6] = own_edge[at : at + 8, :]

    pl.semaphore_wait(barrier, 4)

    def send(src, dst, send_sem, recv_sem, device):
        copy = pltpu.make_async_remote_copy(src, dst, send_sem, recv_sem, device_id=device, device_id_type=MESH)
        copy.start()
        return copy

    to_z = [
        send(zs.at[s], rz.at[s], send_z.at[s], recv_z.at[s], device) for s, device in ((0, z_after), (1, z_before))
    ]
    pieces = (
        (ph_hbm.at[1:8], rx_ph.at[0, 1:8], x_after),
        (ph_hbm.at[0:7], rx_ph.at[1, 0:7], x_before),
        (lam.at[2:8], rx_lam.at[0, 2:8], x_after),
        (lam.at[0:6], rx_lam.at[1, 0:6], x_before),
        (edge_out, ne.at[0:2], x_after),
        (ps.at[0:1], ne.at[2:3], x_before),
        (res.at[3:8], rx_res.at[0, 3:8], x_after),
        (res.at[0:6], rx_res.at[1, 0:6], x_before),
    )
    to_x = []
    for k, (src, dst, device) in enumerate(pieces):
        if k == 99:
            for copy in to_x[0:0]:
                copy.wait_send()
        to_x.append(send(src, dst, send_x.at[k], recv_x.at[k], device))

    inside_x = (w > 0, w < nw - 1)
    inside_z = (n > 0, n < nn - 1)
    to_d = []
    for s in range(2):
        to_z[s].wait_recv()
        at = PAD - 8 if s == 0 else PAD + NZ
        spare = row8 == (0 if s == 0 else 7)
        line = PAD if s == 0 else PAD + NZ - 1
        own_edge[at : at + 8, :] = rz[s, 6]
        for j in range(2):
            phe[2 + j, at : at + 8, :] = jnp.where(inside_z[s], rz[s, 3 * j], 2.0)
            lame[2 + j, at : at + 8, :] = rz[s, 3 * j + 1]
            rese[2 + j, at : at + 8, :] = rz[s, 3 * j + 2]
            pressure = jnp.where(inside_z[s], rz[s, 3 * j + 2], 0.0)
            if s == 0:
                speed = jnp.where(inside_z[s], rz[s, 3 * j + 1], 0.0)
            else:
                speed = vt[2, j, NZ - 1 : NZ, :]
                pe[j, at : at + 1, :] = pressure[7:8, :]
            rz[s, 3 * j + 1] = jnp.where(spare, speed, rz[s, 3 * j + 1])
            rz[s, 3 * j + 2] = jnp.where(spare, pressure - pe[j, line : line + 1, :], rz[s, 3 * j + 2])
        for k, device in ((0, x_after), (1, x_before)):
            to_d.append(send(rz.at[s], rd.at[k, s], send_d.at[k, s], recv_d.at[k, s], device))

    for k in range(2):
        to_x[k].wait_recv()
        for j in range(2):
            block = turned(rx_ph[k, 4 * j : 4 * j + 4].astype(F32))
            phe[4 * k + j, main, :] = jnp.where(inside_x[k], block, 2.0)

    for row in range(PAD, PAD + NZ, 16):
        coefficients(phe, coef, inv, diag, row, 16)

    for k in range(2):
        to_x[2 + k].wait_recv()
        for j in range(2):
            lame[4 * k + j, main, :] = turned(rx_lam[k, 4 * j : 4 * j + 4])
    for k in range(2):
        to_x[4 + k].wait_recv()
    lane128 = lanes(NZ)
    outside = ((lane128 < 64) & jnp.logical_not(inside_x[0])) | (
        (lane128 >= 64) & (lane128 < 96) & jnp.logical_not(inside_x[1])
    )
    near = jnp.where(outside, 0.0, turned(ne[...]))
    near_edge[main, :] = near
    pe[2, main, :] = pltpu.roll(near, 64, 1)
    inner = [(row, 16) for row in range(PAD, PAD + NZ, 16)]
    rims = [(PAD - 8, 16), (PAD + NZ - 8, 16)]
    for row, rows in inner:
        start(lame, inv, coef, near_edge, own_edge, s5, W[5], False, row, rows)
    for m in range(5, 0, -1):
        cotangent_sweep(ss, s_up, coef, m, inner)
    for k in range(2):
        to_x[6 + k].wait_recv()
        for j in range(2):
            rese[4 * k + j, main, :] = turned(rx_res[k, 4 * j : 4 * j + 4])
    for row, rows in inner:
        start(rese, inv, coef, near_edge, own_edge, e0, W[0], True, row, rows)
    for m in range(5):
        residual_sweep(ee, e_up, coef, m, inner)

    for copy in to_d:
        copy.wait_recv()
    lane = lanes(8)
    for s in range(2):
        at = PAD - 8 if s == 0 else PAD + NZ
        for k in range(2):
            for j in range(2):
                c = 4 * k + j
                phe[c, at : at + 8, :] = jnp.where(jnp.logical_and(inside_x[k], inside_z[s]), rd[k, s, 3 * j], 2.0)
                lame[c, at : at + 8, :] = rd[k, s, 3 * j + 1]
                rese[c, at : at + 8, :] = rd[k, s, 3 * j + 2]
        below = jnp.where(inside_x[0], jnp.where(lane < 32, pltpu.roll(rd[0, s, 6], 64, 1), rd[0, s, 6]), 0.0)
        above = jnp.where(inside_x[1], pltpu.roll(rd[1, s, 6], 64, 1), 0.0)
        near_edge[at : at + 8, :] = jnp.where(
            lane < 64, below, jnp.where(lane < 96, above, own_edge[at : at + 8, :])
        )
    for row, rows in rims:
        coefficients(phe, coef, inv, diag, row, rows)
        start(lame, inv, coef, near_edge, own_edge, s5, W[5], False, row, rows)
        start(rese, inv, coef, near_edge, own_edge, e0, W[0], True, row, rows)

    for s in range(2):
        spare = 0 if s == 0 else 7
        for c in range(6):
            j = c % 2
            rows_from = rz.at[s] if c in (2, 3) else rd.at[0 if c < 2 else 1, s]
            speed = rows_from[3 * j + 1, spare : spare + 1, :]
            step = rows_from[3 * j + 2, spare : spare + 1, :]
            own, other = (PAD, PAD - 1) if s == 0 else (PAD + NZ - 1, PAD + NZ)
            c_own = coef[ZD if s == 0 else ZU, c, own : own + 1, :]
            c_other = coef[ZU if s == 0 else ZD, c, other : other + 1, :]
            sign = -W[5] if s == 0 else W[5]
            ss[5, c, own : own + 1, :] += sign * (c_own * speed)
            ss[5, c, other : other + 1, :] -= sign * (c_other * speed)
            ee[0, c, own : own + 1, :] += W[0] * (c_own * step)
            ee[0, c, other : other + 1, :] -= W[0] * (c_other * step)
    for m in range(5):
        cotangent_sweep(ss, s_up, coef, 5 - m, rims)
        residual_sweep(ee, e_up, coef, m, rims)
    for copy in to_z + to_x[:0] + to_x[0:] + to_d:
        copy.wait_send()


def neighbours(src, coef, tiles, have, row, rows):
    lane = lanes(rows)
    cur = {c: src[c, pl.ds(row, rows), :] for c in have}
    for c in tiles:
        v = cur[c]
        near = [
            x_up(v, cur.get(c + 1), lane),
            x_down(v, cur.get(c - 1), lane),
            y_up(v),
            y_down(v),
            src[c, pl.ds(row + 1, rows), :],
            src[c, pl.ds(row - 1, rows), :],
        ]
        prod = [coef[k, c, pl.ds(row, rows), :] * near[k] for k in range(6)]
        yield c, v, near, (prod[0] + prod[1]) + (prod[2] + prod[3]) + (prod[4] + prod[5])


EVERY, MIDDLE = range(6), range(1, 5)


def sweep(src, dst, up, coef, tiles, have, keep, scale, places):
    for row, rows in places:
        for c, v, near, total in neighbours(src, coef, tiles, have, row, rows):
            dst[c, pl.ds(row, rows), :] = keep * v + scale * total
            if c in (2, 3):
                up[0, c - 2, pl.ds(row, rows), :] = near[XU]
                up[1, c - 2, pl.ds(row, rows), :] = near[YU]


def cotangent_sweep(ss, s_up, coef, m, places):
    sweep(
        ss.at[m], ss.at[m - 1], s_up.at[m - 1], coef, EVERY if m == 5 else MIDDLE, EVERY if m >= 4 else MIDDLE,
        W[m - 1] / W[m] * (1.0 - W[m]), W[m - 1], places,
    )


def residual_sweep(ee, e_up, coef, m, places):
    tiles = (range(1, 6), MIDDLE, MIDDLE, MIDDLE, range(2, 5))[m]
    have = (EVERY, range(1, 6), MIDDLE, MIDDLE, MIDDLE)[m]
    sweep(ee.at[m], ee.at[m + 1], e_up.at[m], coef, tiles, have, W[m + 1] / W[m] * (1.0 - W[m]), W[m + 1], places)


def gradients(coef, ss, ee, s_up, e_up, pe, diag, vt, gd_hbm, gp_hbm, gf_hbm, rr, out, gd, gp, gf, sem):
    for c in range(2, 5):
        for row in range(PAD, PAD + NZ + 8, 8):
            at = slice(row, row + 8)
            total = None
            for m in range(6):
                term = ss[m, c, at, :] * ee[m, c, at, :] * (1.0 / W[m])
                total = term if total is None else total + term
            rr[c - 2, at, :] = total
    lane = lanes(8)
    last = (lane & 31) == 31
    copies = []

    def give(src, dst):
        copy = pltpu.make_async_copy(src, dst, sem.at[len(copies)])
        copy.start()
        copies.append(copy)

    for j in range(2):
        c = 2 + j
        for row in range(PAD, PAD + NZ, 8):
            at, next_at, own = slice(row, row + 8), slice(row + 1, row + 9), slice(row - PAD, row - PAD + 8)

            def rises(v, x_next, y_next, z_next):
                return v - x_next, v - jnp.where(last, 0.0, y_next), v - z_next

            p = pe[j, at, :]
            rise = rises(p, x_up(p, pe[j + 1, at, :], lane), y_up(p), pe[j, next_at, :])
            ((_, v, near, total),) = neighbours(ss.at[0], coef, (c,), range(c - 1, c + 2), row, 8)
            out[1, j, own, :] = diag[j, at, :] * ((1.0 / W[0] - 1.0) * v + total)
            source = v
            fall = rises(v, near[XU], near[YU], near[ZU])
            grads = [f * r for f, r in zip(fall, rise)]
            for m in range(1, 6):
                v = ee[m - 1, c, at, :]
                step = rises(v, e_up[m - 1, 0, j, at, :], e_up[m - 1, 1, j, at, :], ee[m - 1, c, next_at, :])
                rise = [r + d for r, d in zip(rise, step)]
                v = ss[m, c, at, :]
                source = source + v
                fall = rises(v, s_up[m - 1, 0, j, at, :], s_up[m - 1, 1, j, at, :], ss[m, c, next_at, :])
                grads = [g + f * r for g, f, r in zip(grads, fall, rise)]
            v = ee[5, c, at, :]
            step = rises(v, x_up(v, ee[5, c + 1, at, :], lane), y_up(v), ee[5, c, next_at, :])
            rise = [r + d for r, d in zip(rise, step)]
            out[0, j, own, :] = source
            v = rr[j, at, :]
            up = (x_up(v, rr[j + 1, at, :], lane), jnp.where(last, 0.0, y_up(v)), rr[j, next_at, :])
            for a in range(3):
                out[2 + a, j, own, :] = vt[a, j, own, :] * rise[a] - grads[a] - (v + up[a])
        part = slice(4 * j, 4 * j + 4)
        gd[part] = jnp.transpose(out[0, j]).reshape(4, NY, NZ)
        give(gd.at[part], gd_hbm.at[part])
        gp[part] = jnp.transpose(out[1, j]).reshape(4, NY, NZ)
        give(gp.at[part], gp_hbm.at[part])
        for a in range(3):
            gf[a, part] = jnp.transpose(out[2 + a, j]).reshape(4, NY, NZ)
            give(gf.at[a, part], gf_hbm.at[a, part])
    for copy in copies:
        copy.wait()


def per_device(divergence, pressure_start, phase, velocity_cot):
    shape = jax.ShapeDtypeStruct
    vmem = pl.BlockSpec(memory_space=pltpu.VMEM)
    dma = pltpu.SemaphoreType.DMA
    args = [
        pltpu.with_memory_space_constraint(a, pltpu.HBM)
        for a in (divergence, pressure_start, phase, velocity_cot)
    ]
    block, tiles = (8, NY, NZ), (6, ROWS, 128)
    made = pl.pallas_call(
        exchange,
        out_shape=[
            shape((6, *tiles), F32),
            shape((6, *tiles), F32),
            shape((6, *tiles), F32),
            shape((5, 2, 2, ROWS, 128), F32),
            shape((5, 2, 2, ROWS, 128), F32),
            shape((3, ROWS, 128), F32),
            shape((2, ROWS, 128), F32),
            shape((3, 2, NZ, 128), F32),
        ],
        in_specs=[pl.BlockSpec(memory_space=pltpu.HBM)] * 4,
        out_specs=[vmem] * 8,
        scratch_shapes=[
            pltpu.VMEM(block, jnp.int32),
            pltpu.VMEM(block, F32),
            pltpu.VMEM(block, F32),
            pltpu.VMEM((3, *block), F32),
            pltpu.VMEM(block, F32),
            pltpu.VMEM(block, F32),
            pltpu.VMEM((2, *block), jnp.int32),
            pltpu.VMEM((2, *block), F32),
            pltpu.VMEM((2, *block), F32),
            pltpu.VMEM((4, NY, NZ), F32),
            pltpu.VMEM((2, NY, NZ), F32),
            pltpu.VMEM((2, 7, 8, 128), F32),
            pltpu.VMEM((2, 7, 8, 128), F32),
            pltpu.VMEM((2, 2, 7, 8, 128), F32),
            pltpu.VMEM(tiles, F32),
            pltpu.VMEM(tiles, F32),
            pltpu.VMEM(tiles, F32),
            pltpu.VMEM(tiles, F32),
            pltpu.VMEM((ROWS, 128), F32),
            pltpu.VMEM((ROWS, 128), F32),
            dma((4,)),
            dma((8,)),
            dma((8,)),
            dma((2,)),
            dma((2,)),
            dma((2, 2)),
            dma((2, 2)),
        ],
        compiler_params=pltpu.CompilerParams(
            collective_id=0, has_side_effects=True, vmem_limit_bytes=24 << 20
        ),
        name="exchange",
    )(*args)
    return tuple(
        pl.pallas_call(
            gradients,
            out_shape=[shape(block, F32), shape(block, F32), shape((3, *block), F32)],
            in_specs=[vmem] * 8,
            out_specs=[pl.BlockSpec(memory_space=pltpu.HBM)] * 3,
            scratch_shapes=[
                pltpu.VMEM((3, ROWS, 128), F32),
                pltpu.VMEM((5, 2, NZ, 128), F32),
                pltpu.VMEM(block, F32),
                pltpu.VMEM(block, F32),
                pltpu.VMEM((3, *block), F32),
                dma((10,)),
            ],
            compiler_params=pltpu.CompilerParams(vmem_limit_bytes=16 << 20),
            name="gradients",
        )(*made)
    )


def solution(mesh):
    field = P("wide", None, "narrow")
    faces = P(None, "wide", None, "narrow")
    return jax.shard_map(
        per_device,
        mesh=mesh,
        in_specs=(field, field, field, faces),
        out_specs=(field, field, faces),
        check_vma=False,
    )
```

```python
import math

import jax
import jax.numpy as jnp
from jax import lax
from jax.experimental import pallas as pl
from jax.experimental.pallas import tpu as pltpu
from jax.sharding import PartitionSpec as P

SWEEPS = 6
CENTER, RADIUS = 1.125, 0.875
PAD = 16
ROWS = 160
NZ = 128
NY = 32
F32 = jnp.float32
MESH = pl.DeviceIdType.MESH
XU, XD, YU, YD, ZU, ZD = range(6)


def chebyshev_weights():
    roots = [CENTER + RADIUS * math.cos(math.pi * (2 * m + 1) / (2 * SWEEPS)) for m in range(SWEEPS)]
    order = []
    for m in range(SWEEPS // 2):
        order += [m, SWEEPS - 1 - m]
    return [1.0 / roots[m] for m in order]


W = chebyshev_weights()


def lanes(rows):
    return lax.broadcasted_iota(jnp.int32, (rows, 128), 1)


def x_up(tile, after, lane):
    return pltpu.roll(tile if after is None else jnp.where(lane < 32, after, tile), 96, 1)


def x_down(tile, before, lane):
    return pltpu.roll(tile if before is None else jnp.where(lane >= 96, before, tile), 32, 1)


def y_up(tile):
    return pltpu.roll(tile, 127, 1)


def y_down(tile):
    return pltpu.roll(tile, 1, 1)


def turned(block):
    return jnp.transpose(block.reshape(128, 128))


def local_sums(ph, ps, dv, vc, lam, res):
    row = lax.broadcasted_iota(jnp.int32, (NY, NZ), 0)
    lane = lax.broadcasted_iota(jnp.int32, (NY, NZ), 1)
    top, bottom, inner = row == NY - 1, row == 0, lane < NZ - 1
    before_lam = before_res = None
    here = ph[0].astype(F32)
    for x in range(8):
        a = here
        base, slope = 1.0 + 0.6 * a, 0.6 + 1.8 * a
        p = ps[x]
        face_y = base + slope * jnp.where(top, a, pltpu.roll(a, NY - 1, 0))
        face_z = jnp.where(inner, base + slope * pltpu.roll(a, NZ - 1, 1), 0.0)
        flux_y = face_y * vc[1, x]
        flux_z = face_z * vc[2, x]
        flow_y = face_y * (p - jnp.where(top, 0.0, pltpu.roll(p, NY - 1, 0)))
        flow_z = face_z * (p - pltpu.roll(p, NZ - 1, 1))
        total = flux_y - jnp.where(bottom, 0.0, pltpu.roll(flux_y, 1, 0)) + flux_z - pltpu.roll(flux_z, 1, 1)
        lower = jnp.where(bottom, -(1.0 + 3.0 * a) * p, pltpu.roll(flow_y, 1, 0))
        rest = dv[x] - (flow_y - lower) - (flow_z - pltpu.roll(flow_z, 1, 1))
        if x > 0:
            total = total - before_lam
            rest = rest + before_res
        if x < 7:
            here = ph[x + 1].astype(F32)
            face_x = base + slope * here
            before_lam = face_x * vc[0, x]
            before_res = face_x * (p - ps[x + 1])
            total = total + before_lam
            rest = rest - before_res
        lam[x] = total
        res[x] = rest


def coefficients(phe, coef, inv, diag, row, rows):
    lane = lanes(rows)
    last, first = (lane & 31) == 31, (lane & 31) == 0
    cur = [phe[c, pl.ds(row, rows), :] for c in range(6)]
    for c in range(6):
        a = cur[c]
        near = [
            x_up(a, cur[c + 1] if c < 5 else None, lane),
            x_down(a, cur[c - 1] if c > 0 else None, lane),
            jnp.where(last, a, y_up(a)),
            jnp.where(first, a, y_down(a)),
            phe[c, pl.ds(row + 1, rows), :],
            phe[c, pl.ds(row - 1, rows), :],
        ]
        near = [b if k in (YU, YD) else jnp.where(b > 1.5, a, b) for k, b in enumerate(near)]
        base, slope = 1.0 + 0.6 * a, 0.6 + 1.8 * a
        total = 6.0 * base + slope * ((near[0] + near[1]) + (near[2] + near[3]) + (near[4] + near[5]))
        inverse = jnp.where(a > 1.5, 0.0, 1.0 / total)
        inv[c, pl.ds(row, rows), :] = inverse
        base, slope = base * inverse, slope * inverse
        for k in range(6):
            value = base + slope * near[k]
            if k == YU:
                value = jnp.where(last, 0.0, value)
            if k == YD:
                value = jnp.where(first, 0.0, value)
            coef[k, c, pl.ds(row, rows), :] = value
        if c in (2, 3):
            diag[c - 2, pl.ds(row, rows), :] = total


def start(right, inv, coef, near_edge, own_edge, dst, scale, residual, row, rows):
    lane = lanes(rows)
    low, high = lane < 32, lane >= 96
    near = near_edge[pl.ds(row, rows), :]
    if residual:
        near = own_edge[pl.ds(row, rows), :] - near
    shifts = (96, 0, 32, 64) if residual else (64, 96, 0, 32)
    for c in range(6):
        value = inv[c, pl.ds(row, rows), :] * right[c, pl.ds(row, rows), :]
        if 1 <= c <= 4:
            face = coef[XU if c in (1, 3) else XD, c, pl.ds(row, rows), :]
            edge = face * (pltpu.roll(near, shifts[c - 1], 1) if shifts[c - 1] else near)
            edge = jnp.where(high if c in (1, 3) else low, edge, 0.0)
            plus = c in (1, 3) if not residual else c in (1, 4)
            value = value + edge if plus else value - edge
        dst[c, pl.ds(row, rows), :] = scale * value


def exchange(
    dv_hbm, ps_hbm, ph_hbm, vc_hbm,
    coef, ss, ee, s_up, e_up, pe, diag, vt,
    ph, ps, dv, vc, lam, res, rx_ph, rx_lam, rx_res, ne, edge_out, zs, rz, rd,
    phe, lame, rese, inv, near_edge, own_edge,
    in_sem, send_x, recv_x, send_z, recv_z, send_d, recv_d,
):
    w, n = lax.axis_index("wide"), lax.axis_index("narrow")
    nw, nn = lax.axis_size("wide"), lax.axis_size("narrow")
    x_after, x_before = (lax.rem(w + 1, nw), n), (lax.rem(w + nw - 1, nw), n)
    z_after, z_before = (w, lax.rem(n + 1, nn)), (w, lax.rem(n + nn - 1, nn))
    s5, e0 = ss.at[5], ee.at[0]
    barrier = pltpu.get_barrier_semaphore()
    inside_x = (w > 0, w < nw - 1)
    inside_z = (n > 0, n < nn - 1)
    partners = ((inside_x[1], x_after), (inside_x[0], x_before), (inside_z[1], z_after), (inside_z[0], z_before))
    for there, device in partners:

        @pl.when(there)
        def _():
            pl.semaphore_signal(barrier, inc=1, device_id=device, device_id_type=MESH)

    loads = [
        pltpu.make_async_copy(src, dst, in_sem.at[k])
        for k, (src, dst) in enumerate(((ph_hbm, ph), (ps_hbm, ps), (dv_hbm, dv), (vc_hbm, vc)))
    ]
    for load in loads:
        load.start()
    zero = jnp.zeros((NY, NZ), F32)
    rx_ph[0, 0] = jnp.zeros((NY, NZ), jnp.int32)
    rx_ph[1, 7] = jnp.zeros((NY, NZ), jnp.int32)
    for k in (0, 1):
        rx_lam[0, k] = zero
        rx_res[0, k] = zero
        rx_lam[1, 6 + k] = zero
        rx_res[1, 6 + k] = zero
    rx_res[0, 2] = zero
    for c in range(6):
        for r in (0, PAD + NZ):
            phe[c, r : r + PAD, :] = jnp.zeros((PAD, 128), F32)
            ss[5, c, r : r + PAD, :] = jnp.zeros((PAD, 128), F32)
            ee[0, c, r : r + PAD, :] = jnp.zeros((PAD, 128), F32)
    for k in range(2):

        @pl.when(jnp.logical_not(inside_x[k]))
        def _():
            rx_lam[k] = jnp.zeros((8, NY, NZ), F32)
            rx_res[k] = jnp.zeros((8, NY, NZ), F32)
            rd[k] = jnp.zeros((2, 7, 8, 128), F32)

        @pl.when(jnp.logical_not(inside_z[k]))
        def _():
            rz[k] = jnp.zeros((7, 8, 128), F32)

    for load in loads:
        load.wait()

    local_sums(ph, ps, dv, vc, lam, res)
    main = slice(PAD, PAD + NZ)
    for j in range(2):
        part = slice(4 * j, 4 * j + 4)
        phe[2 + j, main, :] = turned(ph[part].astype(F32))
        lame[2 + j, main, :] = turned(lam[part])
        rese[2 + j, main, :] = turned(res[part])
        pe[j, main, :] = turned(ps[part])
        for a in range(3):
            vt[a, j] = turned(vc[a, part])
    own_edge[main, :] = turned(jnp.stack([ps[0], vc[0, 7], ps[7], vc[0, 7]]))
    edge_out[0] = ps[7]
    edge_out[1] = vc[0, 7]
    ne[3] = vc[0, 7]
    row8 = lax.broadcasted_iota(jnp.int32, (8, 128), 0)
    for side, at in ((0, PAD + NZ - 8), (1, PAD)):
        for j in range(2):
            spare = row8 == (0 if side == 0 else 7)
            line = PAD + NZ - 1 if side == 0 else PAD
            zs[side, 3 * j] = phe[2 + j, at : at + 8, :]
            zs[side, 3 * j + 1] = jnp.where(spare, vt[2, j, NZ - 1 : NZ, :], lame[2 + j, at : at + 8, :])
            zs[side, 3 * j + 2] = jnp.where(spare, pe[j, line : line + 1, :], rese[2 + j, at : at + 8, :])
        zs[side, 6] = own_edge[at : at + 8, :]

    pl.semaphore_wait(barrier, 4 - jnp.where(w == 0, 1, 0) - jnp.where(w == nw - 1, 1, 0) - jnp.where(n == 0, 1, 0) - jnp.where(n == nn - 1, 1, 0))

    def remote(src, dst, send_sem, recv_sem, device):
        return pltpu.make_async_remote_copy(src, dst, send_sem, recv_sem, device_id=device, device_id_type=MESH)

    to_z = [remote(zs.at[s], rz.at[s], send_z.at[s], recv_z.at[s], device) for s, device in ((0, z_after), (1, z_before))]
    pieces = (
        (ph_hbm.at[1:8], rx_ph.at[0, 1:8], x_after),
        (ph_hbm.at[0:7], rx_ph.at[1, 0:7], x_before),
        (lam.at[2:8], rx_lam.at[0, 2:8], x_after),
        (lam.at[0:6], rx_lam.at[1, 0:6], x_before),
        (edge_out, ne.at[0:2], x_after),
        (ps.at[0:1], ne.at[2:3], x_before),
        (res.at[3:8], rx_res.at[0, 3:8], x_after),
        (res.at[0:6], rx_res.at[1, 0:6], x_before),
    )
    to_x = [remote(src, dst, send_x.at[k], recv_x.at[k], device) for k, (src, dst, device) in enumerate(pieces)]
    to_d = [
        remote(rz.at[s], rd.at[k, s], send_d.at[k, s], recv_d.at[k, s], device)
        for s in range(2)
        for k, device in ((0, x_after), (1, x_before))
    ]

    def act(copies, inside, side, what):
        @pl.when(inside[side])
        def _():
            for copy in copies:
                what(copy)

    def start_all(copies, inside):
        act(copies[0::2], inside, 1, lambda copy: copy.start())
        act(copies[1::2], inside, 0, lambda copy: copy.start())

    def sent(copies, inside):
        act(copies[0::2], inside, 1, lambda copy: copy.wait_send())
        act(copies[1::2], inside, 0, lambda copy: copy.wait_send())

    def received(copy, inside, side):
        act([copy], inside, side, lambda copy: copy.wait_recv())

    start_all(to_z, inside_z)
    start_all(to_x, inside_x)

    for s in range(2):
        received(to_z[s], inside_z, s)
        at = PAD - 8 if s == 0 else PAD + NZ
        spare = row8 == (0 if s == 0 else 7)
        line = PAD if s == 0 else PAD + NZ - 1
        own_edge[at : at + 8, :] = rz[s, 6]
        for j in range(2):
            phe[2 + j, at : at + 8, :] = jnp.where(inside_z[s], rz[s, 3 * j], 2.0)
            lame[2 + j, at : at + 8, :] = rz[s, 3 * j + 1]
            rese[2 + j, at : at + 8, :] = rz[s, 3 * j + 2]
            pressure = jnp.where(inside_z[s], rz[s, 3 * j + 2], 0.0)
            if s == 0:
                speed = jnp.where(inside_z[s], rz[s, 3 * j + 1], 0.0)
            else:
                speed = vt[2, j, NZ - 1 : NZ, :]
                pe[j, at : at + 1, :] = pressure[7:8, :]
            rz[s, 3 * j + 1] = jnp.where(spare, speed, rz[s, 3 * j + 1])
            rz[s, 3 * j + 2] = jnp.where(spare, pressure - pe[j, line : line + 1, :], rz[s, 3 * j + 2])
        start_all(to_d[2 * s : 2 * s + 2], inside_x)

    for k in range(2):
        received(to_x[k], inside_x, k)
        for j in range(2):
            block = turned(rx_ph[k, 4 * j : 4 * j + 4].astype(F32))
            phe[4 * k + j, main, :] = jnp.where(inside_x[k], block, 2.0)

    for row in range(PAD, PAD + NZ, 16):
        coefficients(phe, coef, inv, diag, row, 16)

    for k in range(2):
        received(to_x[2 + k], inside_x, k)
        for j in range(2):
            lame[4 * k + j, main, :] = turned(rx_lam[k, 4 * j : 4 * j + 4])
    for k in range(2):
        received(to_x[4 + k], inside_x, k)
    lane128 = lanes(NZ)
    outside = ((lane128 < 64) & jnp.logical_not(inside_x[0])) | (
        (lane128 >= 64) & (lane128 < 96) & jnp.logical_not(inside_x[1])
    )
    near = jnp.where(outside, 0.0, turned(ne[...]))
    near_edge[main, :] = near
    pe[2, main, :] = pltpu.roll(near, 64, 1)
    inner = [(row, 16) for row in range(PAD, PAD + NZ, 16)]
    rims = [(PAD - 8, 16), (PAD + NZ - 8, 16)]
    for row, rows in inner:
        start(lame, inv, coef, near_edge, own_edge, s5, W[5], False, row, rows)
    for m in range(5, 0, -1):
        cotangent_sweep(ss, s_up, coef, m, inner)
    for k in range(2):
        received(to_x[6 + k], inside_x, k)
        for j in range(2):
            rese[4 * k + j, main, :] = turned(rx_res[k, 4 * j : 4 * j + 4])
    for row, rows in inner:
        start(rese, inv, coef, near_edge, own_edge, e0, W[0], True, row, rows)
    for m in range(5):
        residual_sweep(ee, e_up, coef, m, inner)

    for k in range(2):
        received(to_d[k], inside_x, k)
        received(to_d[2 + k], inside_x, k)
    lane = lanes(8)
    for s in range(2):
        at = PAD - 8 if s == 0 else PAD + NZ
        for k in range(2):
            for j in range(2):
                c = 4 * k + j
                phe[c, at : at + 8, :] = jnp.where(jnp.logical_and(inside_x[k], inside_z[s]), rd[k, s, 3 * j], 2.0)
                lame[c, at : at + 8, :] = rd[k, s, 3 * j + 1]
                rese[c, at : at + 8, :] = rd[k, s, 3 * j + 2]
        below = jnp.where(inside_x[0], jnp.where(lane < 32, pltpu.roll(rd[0, s, 6], 64, 1), rd[0, s, 6]), 0.0)
        above = jnp.where(inside_x[1], pltpu.roll(rd[1, s, 6], 64, 1), 0.0)
        near_edge[at : at + 8, :] = jnp.where(
            lane < 64, below, jnp.where(lane < 96, above, own_edge[at : at + 8, :])
        )
    for row, rows in rims:
        coefficients(phe, coef, inv, diag, row, rows)
        start(lame, inv, coef, near_edge, own_edge, s5, W[5], False, row, rows)
        start(rese, inv, coef, near_edge, own_edge, e0, W[0], True, row, rows)

    for s in range(2):
        spare = 0 if s == 0 else 7
        for c in range(6):
            j = c % 2
            rows_from = rz.at[s] if c in (2, 3) else rd.at[0 if c < 2 else 1, s]
            speed = rows_from[3 * j + 1, spare : spare + 1, :]
            step = rows_from[3 * j + 2, spare : spare + 1, :]
            own, other = (PAD, PAD - 1) if s == 0 else (PAD + NZ - 1, PAD + NZ)
            c_own = coef[ZD if s == 0 else ZU, c, own : own + 1, :]
            c_other = coef[ZU if s == 0 else ZD, c, other : other + 1, :]
            sign = -W[5] if s == 0 else W[5]
            ss[5, c, own : own + 1, :] += sign * (c_own * speed)
            ss[5, c, other : other + 1, :] -= sign * (c_other * speed)
            ee[0, c, own : own + 1, :] += W[0] * (c_own * step)
            ee[0, c, other : other + 1, :] -= W[0] * (c_other * step)
    for m in range(5):
        cotangent_sweep(ss, s_up, coef, 5 - m, rims)
        residual_sweep(ee, e_up, coef, m, rims)
    sent(to_z, inside_z)
    sent(to_x, inside_x)
    sent(to_d, inside_x)


def neighbours(src, coef, tiles, have, row, rows):
    lane = lanes(rows)
    cur = {c: src[c, pl.ds(row, rows), :] for c in have}
    for c in tiles:
        v = cur[c]
        near = [
            x_up(v, cur.get(c + 1), lane),
            x_down(v, cur.get(c - 1), lane),
            y_up(v),
            y_down(v),
            src[c, pl.ds(row + 1, rows), :],
            src[c, pl.ds(row - 1, rows), :],
        ]
        prod = [coef[k, c, pl.ds(row, rows), :] * near[k] for k in range(6)]
        yield c, v, near, (prod[0] + prod[1]) + (prod[2] + prod[3]) + (prod[4] + prod[5])


EVERY, MIDDLE = range(6), range(1, 5)


def sweep(src, dst, up, coef, tiles, have, keep, scale, places):
    for row, rows in places:
        for c, v, near, total in neighbours(src, coef, tiles, have, row, rows):
            dst[c, pl.ds(row, rows), :] = keep * v + scale * total
            if c in (2, 3):
                up[0, c - 2, pl.ds(row, rows), :] = near[XU]
                up[1, c - 2, pl.ds(row, rows), :] = near[YU]


def cotangent_sweep(ss, s_up, coef, m, places):
    sweep(
        ss.at[m], ss.at[m - 1], s_up.at[m - 1], coef, EVERY if m == 5 else MIDDLE, EVERY if m >= 4 else MIDDLE,
        W[m - 1] / W[m] * (1.0 - W[m]), W[m - 1], places,
    )


def residual_sweep(ee, e_up, coef, m, places):
    tiles = (range(1, 6), MIDDLE, MIDDLE, MIDDLE, range(2, 5))[m]
    have = (EVERY, range(1, 6), MIDDLE, MIDDLE, MIDDLE)[m]
    sweep(ee.at[m], ee.at[m + 1], e_up.at[m], coef, tiles, have, W[m + 1] / W[m] * (1.0 - W[m]), W[m + 1], places)


def gradients(coef, ss, ee, s_up, e_up, pe, diag, vt, gd_hbm, gp_hbm, gf_hbm, rr, out, gd, gp, gf, sem):
    for c in range(2, 5):
        for row in range(PAD, PAD + NZ + 8, 8):
            at = slice(row, row + 8)
            total = None
            for m in range(6):
                term = ss[m, c, at, :] * ee[m, c, at, :] * (1.0 / W[m])
                total = term if total is None else total + term
            rr[c - 2, at, :] = total
    lane = lanes(8)
    last = (lane & 31) == 31
    copies = []

    def give(src, dst):
        copy = pltpu.make_async_copy(src, dst, sem.at[len(copies)])
        copy.start()
        copies.append(copy)

    for j in range(2):
        c = 2 + j
        for row in range(PAD, PAD + NZ, 8):
            at, next_at, own = slice(row, row + 8), slice(row + 1, row + 9), slice(row - PAD, row - PAD + 8)

            def rises(v, x_next, y_next, z_next):
                return v - x_next, v - jnp.where(last, 0.0, y_next), v - z_next

            p = pe[j, at, :]
            rise = rises(p, x_up(p, pe[j + 1, at, :], lane), y_up(p), pe[j, next_at, :])
            ((_, v, near, total),) = neighbours(ss.at[0], coef, (c,), range(c - 1, c + 2), row, 8)
            out[1, j, own, :] = diag[j, at, :] * ((1.0 / W[0] - 1.0) * v + total)
            source = v
            fall = rises(v, near[XU], near[YU], near[ZU])
            grads = [f * r for f, r in zip(fall, rise)]
            for m in range(1, 6):
                v = ee[m - 1, c, at, :]
                step = rises(v, e_up[m - 1, 0, j, at, :], e_up[m - 1, 1, j, at, :], ee[m - 1, c, next_at, :])
                rise = [r + d for r, d in zip(rise, step)]
                v = ss[m, c, at, :]
                source = source + v
                fall = rises(v, s_up[m - 1, 0, j, at, :], s_up[m - 1, 1, j, at, :], ss[m, c, next_at, :])
                grads = [g + f * r for g, f, r in zip(grads, fall, rise)]
            v = ee[5, c, at, :]
            step = rises(v, x_up(v, ee[5, c + 1, at, :], lane), y_up(v), ee[5, c, next_at, :])
            rise = [r + d for r, d in zip(rise, step)]
            out[0, j, own, :] = source
            v = rr[j, at, :]
            up = (x_up(v, rr[j + 1, at, :], lane), jnp.where(last, 0.0, y_up(v)), rr[j, next_at, :])
            for a in range(3):
                out[2 + a, j, own, :] = vt[a, j, own, :] * rise[a] - grads[a] - (v + up[a])
        part = slice(4 * j, 4 * j + 4)
        gd[part] = jnp.transpose(out[0, j]).reshape(4, NY, NZ)
        give(gd.at[part], gd_hbm.at[part])
        gp[part] = jnp.transpose(out[1, j]).reshape(4, NY, NZ)
        give(gp.at[part], gp_hbm.at[part])
        for a in range(3):
            gf[a, part] = jnp.transpose(out[2 + a, j]).reshape(4, NY, NZ)
            give(gf.at[a, part], gf_hbm.at[a, part])
    for copy in copies:
        copy.wait()


def per_device(divergence, pressure_start, phase, velocity_cot):
    shape = jax.ShapeDtypeStruct
    vmem = pl.BlockSpec(memory_space=pltpu.VMEM)
    dma = pltpu.SemaphoreType.DMA
    args = [
        pltpu.with_memory_space_constraint(a, pltpu.HBM)
        for a in (divergence, pressure_start, phase, velocity_cot)
    ]
    block, tiles = (8, NY, NZ), (6, ROWS, 128)
    made = pl.pallas_call(
        exchange,
        out_shape=[
            shape((6, *tiles), F32),
            shape((6, *tiles), F32),
            shape((6, *tiles), F32),
            shape((5, 2, 2, ROWS, 128), F32),
            shape((5, 2, 2, ROWS, 128), F32),
            shape((3, ROWS, 128), F32),
            shape((2, ROWS, 128), F32),
            shape((3, 2, NZ, 128), F32),
        ],
        in_specs=[pl.BlockSpec(memory_space=pltpu.HBM)] * 4,
        out_specs=[vmem] * 8,
        scratch_shapes=[
            pltpu.VMEM(block, jnp.int32),
            pltpu.VMEM(block, F32),
            pltpu.VMEM(block, F32),
            pltpu.VMEM((3, *block), F32),
            pltpu.VMEM(block, F32),
            pltpu.VMEM(block, F32),
            pltpu.VMEM((2, *block), jnp.int32),
            pltpu.VMEM((2, *block), F32),
            pltpu.VMEM((2, *block), F32),
            pltpu.VMEM((4, NY, NZ), F32),
            pltpu.VMEM((2, NY, NZ), F32),
            pltpu.VMEM((2, 7, 8, 128), F32),
            pltpu.VMEM((2, 7, 8, 128), F32),
            pltpu.VMEM((2, 2, 7, 8, 128), F32),
            pltpu.VMEM(tiles, F32),
            pltpu.VMEM(tiles, F32),
            pltpu.VMEM(tiles, F32),
            pltpu.VMEM(tiles, F32),
            pltpu.VMEM((ROWS, 128), F32),
            pltpu.VMEM((ROWS, 128), F32),
            dma((4,)),
            dma((8,)),
            dma((8,)),
            dma((2,)),
            dma((2,)),
            dma((2, 2)),
            dma((2, 2)),
        ],
        compiler_params=pltpu.CompilerParams(
            collective_id=0, has_side_effects=True, vmem_limit_bytes=24 << 20
        ),
        name="exchange",
    )(*args)
    return tuple(
        pl.pallas_call(
            gradients,
            out_shape=[shape(block, F32), shape(block, F32), shape((3, *block), F32)],
            in_specs=[vmem] * 8,
            out_specs=[pl.BlockSpec(memory_space=pltpu.HBM)] * 3,
            scratch_shapes=[
                pltpu.VMEM((3, ROWS, 128), F32),
                pltpu.VMEM((5, 2, NZ, 128), F32),
                pltpu.VMEM(block, F32),
                pltpu.VMEM(block, F32),
                pltpu.VMEM((3, *block), F32),
                dma((10,)),
            ],
            compiler_params=pltpu.CompilerParams(vmem_limit_bytes=16 << 20),
            name="gradients",
        )(*made)
    )


def solution(mesh):
    field = P("wide", None, "narrow")
    faces = P(None, "wide", None, "narrow")
    return jax.shard_map(
        per_device,
        mesh=mesh,
        in_specs=(field, field, field, faces),
        out_specs=(field, field, faces),
        check_vma=False,
    )
```
